32 devices in a mesh: dp: 8 (over z, core), expert: 4 (over y, x).
Axes of the slice: x: 2, y: 2, z: 4, core: 2. Of those that a mesh axis runs over, the one named last changes fastest.
Arguments:
- tokens: bfloat16 [8192, 1024], P(('dp', 'expert')), may hold values from -6 to 6
- router: bfloat16 [1024, 4], replicated, may hold values from -0.1875 to 0.1875
- w_in: bfloat16 [4, 1024, 2048], P('expert'), may hold values from -0.1875 to 0.1875
- w_out: bfloat16 [4, 2048, 1024], P('expert'), may hold values from -0.125 to 0.125
- assign: int32 [8192], P(('dp', 'expert')), may hold values from 0 to 3, as said below
- modality: int32 [8192], P(('dp', 'expert')), may hold values from 0 to 1
- slot: int32 [8192], P(('dp', 'expert')), may hold values from 0 to 95, as said below
Outputs:
- mixed: bfloat16 [8192, 1024], P(('dp', 'expert'))
- importance: float32 [2, 4], replicated
- entropies: float32 [2, 2], replicated
The draws below stay inside these ranges and needn't reach their ends.
Inputs may be any that keep to these rules, and one draw needn't show every extreme that they name: `assign`: in the rows of one device each expert is named at most 96 times; in every device's rows one expert is named exactly 96 times, the same expert for all devices of one index of dp. A token's slot is the number of earlier rows of the same device that name the same expert.
All inputs are finite; a program needn't handle non-finite values.
Results may differ from the reference program's by a relative error of at most 0.003.
The reference program's roundings to bfloat16 on the way count: a program that leaves them out, or rounds other values in their place, can miss the bound.
Values may be sent and summed in bfloat16 or wider, within the bound.
A program may use at most 64 MiB of HBM per device.

```python
import jax
import jax.numpy as jnp
from jax import lax

D = 1024
FF = 2048
TOK_DEV = 256
EXPERTS = 4
CAP = 96
TOKENS = 8192
N_EXPERT = 4
DEVICES = 32


def joint_routes(key):
    base = jax.random.fold_in(key, 11)
    count = TOKENS // TOK_DEV

    def one_block(index):
        block_key = jax.random.fold_in(base, index)
        row_key = jax.random.fold_in(jax.random.fold_in(base, 100003), index // N_EXPERT)
        filled = jax.random.randint(row_key, (), 0, EXPERTS)
        shuffled = jax.random.permutation(jax.random.fold_in(block_key, 1), EXPERTS * CAP)
        order = jnp.argsort((shuffled // CAP != filled).astype(jnp.int32), stable=True)
        chosen = shuffled[order][:TOK_DEV]
        labels = jax.random.permutation(jax.random.fold_in(block_key, 2), chosen)
        experts_of = (labels // CAP).astype(jnp.int32)
        onehot = (experts_of[:, None] == jnp.arange(EXPERTS, dtype=jnp.int32)[None, :]).astype(jnp.int32)
        before = jnp.cumsum(onehot, axis=0) - onehot
        ranks = jnp.sum(before * onehot, axis=1).astype(jnp.int32)
        return (experts_of, ranks)
    experts_all, ranks_all = jax.vmap(one_block)(jnp.arange(count))
    return (experts_all.reshape(-1).astype(jnp.int32), ranks_all.reshape(-1).astype(jnp.int32))


def draw_assign(key, part):
    return joint_routes(key)[0].astype(jnp.int32)


def draw_slot(key, part):
    return joint_routes(key)[1].astype(jnp.int32)


def with_ends(entries, stream_key, least, largest):
    longest = entries.shape.index(max(entries.shape))
    spots = []
    for shift in (0, 1):
        where = [jax.random.randint(jax.random.fold_in(stream_key, axis), (), 0, length) for axis, length in enumerate(entries.shape)]
        where[longest] = (where[longest] + shift) % entries.shape[longest]
        spots.append(tuple(where))
    return entries.at[spots[0]].set(least).at[spots[1]].set(largest)


def shard_levels(key, extent, split, low, high):
    level, own = 1.0, jax.random.fold_in(key, 6)
    for dim, blocks in split:
        draws = jnp.exp(jax.random.uniform(jax.random.fold_in(own, dim), (blocks,), jnp.float32, low / len(split), high / len(split)))
        level = level * jnp.repeat(draws, extent[dim] // blocks).reshape([-1 if axis == dim else 1 for axis in range(len(extent))])
    return level


def bell_draw(rng, shape, spread, limit, shards=(), held_as=jnp.bfloat16):
    factor_of = shard_levels(rng, shape, shards, -0.22, 0.18) if shards else 1.0
    values = jax.random.normal(rng, shape, jnp.float32) * spread * factor_of
    return jnp.minimum(jnp.maximum(values, -limit), limit).astype(held_as)


def setup_inputs(seed: int = 0) -> dict:
    seeds = jax.random.split(jax.random.key(seed), 8)
    tokens = bell_draw(seeds[0], (TOKENS, D), 1.0, 6.0, ((0, 32),))
    router = bell_draw(seeds[1], (D, EXPERTS), D ** -0.5, 0.1875)
    w_in = bell_draw(seeds[2], (EXPERTS, D, FF), D ** -0.5, 0.1875, ((0, 4),))
    w_out = bell_draw(seeds[3], (EXPERTS, FF, D), FF ** -0.5, 0.125, ((0, 4),))
    assign = draw_assign(jax.random.fold_in(seeds[7], 71), 0)
    modality = with_ends(jax.random.randint(seeds[5], (TOKENS,), 0, 2), jax.random.fold_in(seeds[5], 1), 0, 1).astype(jnp.int32)
    slot = draw_slot(jax.random.fold_in(seeds[7], 71), 0)
    return dict(tokens=tokens, router=router, w_in=w_in, w_out=w_out, assign=assign, modality=modality, slot=slot)


def expert_rows(pair):
    rows, first, second = pair
    hidden = jax.nn.gelu(jnp.dot(rows, first, preferred_element_type=jnp.float32)).astype(jnp.bfloat16)
    return jnp.dot(hidden, second, preferred_element_type=jnp.float32).astype(jnp.bfloat16)


def reference(tokens, router, w_in, w_out, assign, modality, slot):
    logits = jnp.dot(tokens, router, preferred_element_type=jnp.float32)
    probs = jax.nn.softmax(logits, axis=-1)
    logp = jax.nn.log_softmax(logits, axis=-1)
    picked = (assign[:, None] == jnp.arange(EXPERTS, dtype=jnp.int32)[None, :]).astype(jnp.float32)
    gate = jnp.sum(probs * picked, axis=-1)
    token_entropy = -jnp.sum(probs * logp, axis=-1)
    blocks = (jnp.arange(TOKENS, dtype=jnp.int32) // TOK_DEV).astype(jnp.int32)
    position = (blocks * CAP + slot).astype(jnp.int32)
    buffer = jnp.zeros((EXPERTS, DEVICES * CAP, D), jnp.bfloat16).at[assign, position].set(tokens)
    outputs = lax.map(expert_rows, (buffer, w_in, w_out))
    chosen = outputs[assign, position].astype(jnp.float32)
    mixed = (gate[:, None] * chosen).astype(jnp.bfloat16)
    kinds = (modality[:, None] == jnp.arange(2, dtype=jnp.int32)[None, :]).astype(jnp.float32)
    sums = jnp.dot(kinds.T, probs, precision=lax.Precision.HIGHEST)
    counts = jnp.sum(kinds, axis=0)
    ent_sum = jnp.dot(kinds.T, token_entropy, precision=lax.Precision.HIGHEST)
    denom = jnp.maximum(counts, 1.0)
    importance = sums / denom[:, None]
    global_ent = -jnp.sum(jax.scipy.special.xlogy(importance, importance), axis=-1)
    entropies = jnp.stack([ent_sum / denom, global_ent], axis=1)
    return mixed, importance, entropies
```

```python
import functools

import jax
import jax.numpy as jnp
from jax import lax
from jax.experimental import pallas as pl
from jax.experimental.pallas import tpu as pltpu
from jax.sharding import PartitionSpec as P

MESH = pl.DeviceIdType.MESH


def partner(me, k, n):
    out, bit = 0, 1
    while bit < n:
        digit = lax.rem(lax.div(me, bit), 2)
        if k & bit:
            digit = 1 - digit
        out = out + digit * bit
        bit *= 2
    return out


def to_columns(row):
    return jnp.transpose(jnp.broadcast_to(row, (128, row.shape[1])))


def kernel(
    n, n_dp, cap, chunks, tokens_hbm, router_t, w_in_hbm, w_out_hbm, assign, modality, slot,
    mixed, importance, entropies,
    tokens, w1, w2, buf, recv, res, ret, hidden, chosen, stat1, stat2,
    tok_sem, w1_sem, w2_sem, out_send, out_recv, back_send, back_recv, s1_send, s1_recv, s2_send, s2_recv,
):
    me = lax.axis_index("expert")
    me_dp = lax.axis_index("dp")
    peers = [partner(me, k, n) for k in range(n)]
    peers_dp = [partner(me_dp, k, n_dp) for k in range(n_dp)]
    n_tok, width = tokens.shape
    n_exp = router_t.shape[0]
    part = cap // chunks
    span = (n - 1) * part

    tok_copy = pltpu.make_async_copy(tokens_hbm, tokens, tok_sem)
    tok_copy.start()
    barrier = pltpu.get_barrier_semaphore()
    for k in range(1, n):
        pl.semaphore_signal(barrier, inc=1, device_id={"expert": peers[k]}, device_id_type=MESH)
    for k in range(1, n_dp):
        pl.semaphore_signal(barrier, inc=1, device_id={"dp": peers_dp[k]}, device_id_type=MESH)

    n1, n2 = w1.shape[0], w2.shape[0]
    c1, c2 = w1.shape[2], w2.shape[2]

    def w1_copy(j):
        return pltpu.make_async_copy(w_in_hbm.at[0, :, pl.ds(j * c1, c1)], w1.at[j], w1_sem.at[j])

    def w2_copy(j):
        return pltpu.make_async_copy(w_out_hbm.at[0, :, pl.ds(j * c2, c2)], w2.at[j], w2_sem.at[j])

    rel = jnp.bitwise_xor(assign[...], me)
    where_slot = slot[...]
    piece = lax.div(where_slot, part)
    label = jnp.where(
        rel == 0, where_slot, cap + piece * span + (rel - 1) * part + where_slot - piece * part
    )

    def place(start, count):
        rows = lax.broadcasted_iota(jnp.int32, (count, n_tok), 0) + start
        one_hot = jnp.where(rows == label, 1.0, 0.0).astype(jnp.bfloat16)
        buf[start : start + count, :] = jnp.dot(
            one_hot, tokens[...], preferred_element_type=jnp.float32
        ).astype(jnp.bfloat16)

    def rows_of(c, k):
        return pl.ds(cap + c * span + (k - 1) * part, part)

    def send(src, dst, sems, c, k):
        rows = rows_of(c, k)
        return pltpu.make_async_remote_copy(
            src_ref=src.at[rows], dst_ref=dst.at[rows],
            send_sem=sems[0].at[c, k], recv_sem=sems[1].at[c, k],
            device_id={"expert": peers[k]}, device_id_type=MESH,
        )

    def out_copy(c, k):
        return send(buf, recv, (out_send, out_recv), c, k)

    def back_copy(c, k):
        return send(res, ret, (back_send, back_recv), c, k)

    tok_copy.wait()
    for j in range(n1):
        w1_copy(j).start()
    for j in range(n2):
        w2_copy(j).start()
    for c in range(chunks):
        place(cap + c * span, span)
        if c == 0:
            pl.semaphore_wait(barrier, n - 1 + n_dp - 1)
        for k in reversed(range(1, n)):
            out_copy(c, k).start()
    place(0, cap)

    logits = lax.dot_general(
        router_t[...], tokens[...], (((1,), (1,)), ((), ())), preferred_element_type=jnp.float32
    )
    shifted = logits - jnp.max(logits, axis=0, keepdims=True)
    unnorm = jnp.exp(shifted)
    total = jnp.sum(unnorm, axis=0, keepdims=True)
    probs = unnorm / total
    logp = shifted - jnp.log(total)
    picked = lax.broadcasted_iota(jnp.int32, probs.shape, 0) == assign[...]
    gate = jnp.sum(jnp.where(picked, probs, 0.0), axis=0, keepdims=True)
    entropy = -jnp.sum(probs * logp, axis=0, keepdims=True)
    kinds = [(modality[...] == m).astype(jnp.float32) for m in range(2)]

    def by_kind(values):
        first, second = (jnp.sum(values * kind, axis=1, keepdims=True) for kind in kinds)
        lane = lax.broadcasted_iota(jnp.int32, (values.shape[0], 128), 1)
        return jnp.where(lane == 0, first, jnp.where(lane == 1, second, 0.0))

    stat1[me] = jnp.zeros(stat1.shape[1:], jnp.float32)
    stat1[me, 0:n_exp, :] = by_kind(probs)
    stat1[me, n_exp : n_exp + 1, :] = by_kind(jnp.ones_like(gate))
    stat1[me, n_exp + 1 : n_exp + 2, :] = by_kind(entropy)

    def s1_copy(k):
        return pltpu.make_async_remote_copy(
            src_ref=stat1.at[me], dst_ref=stat1.at[me], send_sem=s1_send.at[k],
            recv_sem=s1_recv.at[k], device_id={"expert": peers[k]}, device_id_type=MESH,
        )

    def s2_copy(k):
        return pltpu.make_async_remote_copy(
            src_ref=stat2.at[me_dp], dst_ref=stat2.at[me_dp], send_sem=s2_send.at[k],
            recv_sem=s2_recv.at[k], device_id={"dp": peers_dp[k]}, device_id_type=MESH,
        )

    for k in range(1, n):
        s1_copy(k).start()

    def experts(src, dst, start, count, first):
        @pl.loop(0, n1)
        def _(j):
            if first:
                w1_copy(j).wait()
            act = jax.nn.gelu(
                jnp.dot(src[start : start + count, :], w1[j], preferred_element_type=jnp.float32)
            )
            hidden[0:count, pl.ds(pl.multiple_of(j * c1, c1), c1)] = act.astype(jnp.bfloat16)

        @pl.loop(0, n2)
        def _(j):
            if first:
                w2_copy(j).wait()
            dst[start : start + count, pl.ds(pl.multiple_of(j * c2, c2), c2)] = jnp.dot(
                hidden[0:count, :], w2[j], preferred_element_type=jnp.float32
            ).astype(jnp.bfloat16)

    experts(buf, ret, 0, cap, True)

    for k in range(1, n):
        s1_copy(k).wait()
    stat2[me_dp] = sum(stat1[i] for i in range(n))
    for k in range(1, n_dp):
        s2_copy(k).start()

    for c in range(chunks):
        for k in range(1, n):
            out_copy(c, k).wait_recv()
        experts(recv, res, cap + c * span, span, False)
        for k in reversed(range(1, n)):
            back_copy(c, k).start()

    label_columns = to_columns(label.astype(jnp.float32))
    gate_column = to_columns(gate)[:, 0:1]

    def gather(start, count):
        lanes = lax.broadcasted_iota(jnp.int32, (n_tok, count), 1) + start
        one_hot = jnp.where(lanes.astype(jnp.float32) == label_columns[:, 0:1], 1.0, 0.0)
        return jnp.dot(
            one_hot.astype(jnp.bfloat16), ret[start : start + count, :],
            preferred_element_type=jnp.float32,
        )

    chosen[...] = gather(0, cap)

    for k in range(1, n_dp):
        s2_copy(k).wait()
    totals = jnp.transpose(sum(stat2[i] for i in range(n_dp)))
    denom = jnp.maximum(totals[0:2, n_exp : n_exp + 1], 1.0)
    mean = totals[0:2, 0:n_exp] / denom
    importance[...] = mean
    logs = jnp.log(jnp.where(mean == 0.0, 1.0, mean))
    entropies[:, 0:1] = totals[0:2, n_exp + 1 : n_exp + 2] / denom
    entropies[:, 1:2] = -jnp.sum(mean * logs, axis=1, keepdims=True)

    for c in range(chunks):
        for k in range(1, n):
            back_copy(c, k).wait_recv()
        if c < chunks - 1:
            chosen[...] += gather(cap + c * span, span)
        else:
            mixed[...] = (
                gate_column * (chosen[...] + gather(cap + c * span, span))
            ).astype(jnp.bfloat16)

    for c in range(chunks):
        for k in range(1, n):
            out_copy(c, k).wait_send()
            back_copy(c, k).wait_send()


def per_device(n, n_dp, tokens, router, w_in, w_out, assign, modality, slot):
    n_tok, width = tokens.shape
    n_exp = router.shape[1]
    ff = w_in.shape[2]
    cap = -(-(3 * n_tok // (2 * n_exp)) // 16) * 16
    chunks = 2 if cap % 32 == 0 else 1
    rows = n * cap
    c1, c2 = min(ff, 512), min(width, 256)
    stat_rows = -(-(n_exp + 2) // 8) * 8
    vmem = pl.BlockSpec(memory_space=pltpu.VMEM)
    hbm = pl.BlockSpec(memory_space=pl.ANY)
    dma = pltpu.SemaphoreType.DMA
    block = pltpu.VMEM((rows, width), jnp.bfloat16)
    return pl.pallas_call(
        functools.partial(kernel, n, n_dp, cap, chunks),
        out_shape=(
            jax.ShapeDtypeStruct((n_tok, width), jnp.bfloat16),
            jax.ShapeDtypeStruct((2, n_exp), jnp.float32),
            jax.ShapeDtypeStruct((2, 2), jnp.float32),
        ),
        in_specs=[hbm, vmem, hbm, hbm, vmem, vmem, vmem],
        out_specs=(vmem, vmem, vmem),
        scratch_shapes=[
            pltpu.VMEM((n_tok, width), jnp.bfloat16),
            pltpu.VMEM((ff // c1, width, c1), jnp.bfloat16),
            pltpu.VMEM((width // c2, ff, c2), jnp.bfloat16),
            block, block, block, block,
            pltpu.VMEM((max(cap, rows - cap), ff), jnp.bfloat16),
            pltpu.VMEM((n_tok, width), jnp.float32),
            pltpu.VMEM((n, stat_rows, 128), jnp.float32),
            pltpu.VMEM((n_dp, stat_rows, 128), jnp.float32),
            dma, dma((ff // c1,)), dma((width // c2,)),
            dma((chunks, n)), dma((chunks, n)), dma((chunks, n)), dma((chunks, n)),
            dma((n,)), dma((n,)), dma((n_dp,)), dma((n_dp,)),
        ],
        compiler_params=pltpu.CompilerParams(
            collective_id=0, has_side_effects=True, vmem_limit_bytes=40 * 2**20
        ),
        cost_estimate=pl.CostEstimate(
            flops=4 * rows * width * ff, bytes_accessed=4 * width * ff, transcendentals=rows * ff
        ),
    )(
        tokens, router.T, w_in, w_out,
        assign.reshape(1, n_tok), modality.reshape(1, n_tok), slot.reshape(1, n_tok),
    )


def solution(mesh):
    return jax.shard_map(
        functools.partial(per_device, mesh.shape["expert"], mesh.shape["dp"]),
        mesh=mesh,
        in_specs=(
            P(("dp", "expert"), None),
            P(),
            P("expert", None, None),
            P("expert", None, None),
            P(("dp", "expert")),
            P(("dp", "expert")),
            P(("dp", "expert")),
        ),
        out_specs=(P(("dp", "expert"), None), P(), P()),
        check_vma=False,
    )
```

```python
import functools

import jax
import jax.numpy as jnp
from jax import lax
from jax.experimental import pallas as pl
from jax.experimental.pallas import tpu as pltpu
from jax.sharding import PartitionSpec as P

MESH = pl.DeviceIdType.MESH
VMEM_LIMIT = 63 * 2**20


def partner(me, k, n):
    out, bit = 0, 1
    while bit < n:
        digit = lax.rem(lax.div(me, bit), 2)
        if k & bit:
            digit = 1 - digit
        out = out + digit * bit
        bit *= 2
    return out


def to_columns(row):
    return jnp.transpose(jnp.broadcast_to(row, (128, row.shape[1])))


def kernel(
    n, n_dp, cap, chunks,
    tokens_hbm, router_hbm, w_in_hbm, w_out_hbm, assign_hbm, modality_hbm, slot_hbm,
    mixed_hbm, importance_hbm, entropies_hbm,
    mixed, importance, entropies, tokens, router_t, assign, modality, slot, w1, w2, buf, recv, res, ret, hidden, chosen, stat1, stat2,
    in_sem, out_sem, w1_sem, w2_sem, out_send, out_recv, back_send, back_recv, s1_send, s1_recv, s2_send, s2_recv,
):
    me = lax.axis_index("expert")
    me_dp = lax.axis_index("dp")
    peers = [partner(me, k, n) for k in range(n)]
    peers_dp = [partner(me_dp, k, n_dp) for k in range(n_dp)]
    n_tok, width = tokens.shape
    n_exp = router_t.shape[0]
    part = cap // chunks
    span = (n - 1) * part

    pairs = (
        (assign_hbm, assign), (slot_hbm, slot), (tokens_hbm, tokens),
        (router_hbm, router_t), (modality_hbm, modality),
    )
    loads = [pltpu.make_async_copy(a, b, in_sem.at[i]) for i, (a, b) in enumerate(pairs)]
    for load in loads:
        load.start()
    barrier = pltpu.get_barrier_semaphore()
    for k in range(1, n):
        pl.semaphore_signal(barrier, inc=1, device_id={"expert": peers[k]}, device_id_type=MESH)
    for k in range(1, n_dp):
        pl.semaphore_signal(barrier, inc=1, device_id={"dp": peers_dp[k]}, device_id_type=MESH)

    n1, n2 = w1.shape[0], w2.shape[0]
    c1, c2 = w1.shape[2], w2.shape[2]

    def w1_copy(j):
        return pltpu.make_async_copy(w_in_hbm.at[0, :, pl.ds(j * c1, c1)], w1.at[j], w1_sem.at[j])

    def w2_copy(j):
        return pltpu.make_async_copy(w_out_hbm.at[0, :, pl.ds(j * c2, c2)], w2.at[j], w2_sem.at[j])

    loads[0].wait()
    loads[1].wait()
    rel = jnp.bitwise_xor(assign[...], me)
    where_slot = slot[...]
    piece = lax.div(where_slot, part)
    label = jnp.where(
        rel == 0, where_slot, cap + piece * span + (rel - 1) * part + where_slot - piece * part
    )

    def place(start, count):
        rows = lax.broadcasted_iota(jnp.int32, (count, n_tok), 0) + start
        one_hot = jnp.where(rows == label, 1.0, 0.0).astype(jnp.bfloat16)
        buf[start : start + count, :] = jnp.dot(
            one_hot, tokens[...], preferred_element_type=jnp.float32
        ).astype(jnp.bfloat16)

    def rows_of(c, k):
        return pl.ds(cap + c * span + (k - 1) * part, part)

    def send(src, dst, sems, c, k):
        rows = rows_of(c, k)
        return pltpu.make_async_remote_copy(
            src_ref=src.at[rows], dst_ref=dst.at[rows],
            send_sem=sems[0].at[c, k], recv_sem=sems[1].at[c, k],
            device_id={"expert": peers[k]}, device_id_type=MESH,
        )

    def out_copy(c, k):
        return send(buf, recv, (out_send, out_recv), c, k)

    def back_copy(c, k):
        return send(res, ret, (back_send, back_recv), c, k)

    loads[2].wait()
    for j in range(n1):
        w1_copy(j).start()
    for j in range(n2):
        w2_copy(j).start()
    for c in range(chunks):
        place(cap + c * span, span)
        if c == 0:
            pl.semaphore_wait(barrier, n - 1 + n_dp - 1)
        for k in reversed(range(1, n)):
            out_copy(c, k).start()
    place(0, cap)

    loads[3].wait()
    loads[4].wait()
    logits = lax.dot_general(
        router_t[...], tokens[...], (((1,), (1,)), ((), ())), preferred_element_type=jnp.float32
    )
    shifted = logits - jnp.max(logits, axis=0, keepdims=True)
    unnorm = jnp.exp(shifted)
    total = jnp.sum(unnorm, axis=0, keepdims=True)
    probs = unnorm / total
    logp = shifted - jnp.log(total)
    picked = lax.broadcasted_iota(jnp.int32, probs.shape, 0) == assign[...]
    gate = jnp.sum(jnp.where(picked, probs, 0.0), axis=0, keepdims=True)
    entropy = -jnp.sum(probs * logp, axis=0, keepdims=True)
    kinds = [(modality[...] == m).astype(jnp.float32) for m in range(2)]

    def by_kind(values):
        first, second = (jnp.sum(values * kind, axis=1, keepdims=True) for kind in kinds)
        lane = lax.broadcasted_iota(jnp.int32, (values.shape[0], 128), 1)
        return jnp.where(lane == 0, first, jnp.where(lane == 1, second, 0.0))

    stat1[me] = jnp.zeros(stat1.shape[1:], jnp.float32)
    stat1[me, 0:n_exp, :] = by_kind(probs)
    stat1[me, n_exp : n_exp + 1, :] = by_kind(jnp.ones_like(gate))
    stat1[me, n_exp + 1 : n_exp + 2, :] = by_kind(entropy)

    def s1_copy(k):
        return pltpu.make_async_remote_copy(
            src_ref=stat1.at[me], dst_ref=stat1.at[me], send_sem=s1_send.at[k],
            recv_sem=s1_recv.at[k], device_id={"expert": peers[k]}, device_id_type=MESH,
        )

    def s2_copy(k):
        return pltpu.make_async_remote_copy(
            src_ref=stat2.at[me_dp], dst_ref=stat2.at[me_dp], send_sem=s2_send.at[k],
            recv_sem=s2_recv.at[k], device_id={"dp": peers_dp[k]}, device_id_type=MESH,
        )

    for k in range(1, n):
        s1_copy(k).start()

    def experts(src, dst, start, count, first):
        for j in range(n1):
            if first:
                w1_copy(j).wait()
            act = jax.nn.gelu(
                jnp.dot(src[start : start + count, :], w1[j], preferred_element_type=jnp.float32)
            )
            hidden[0:count, pl.ds(j * c1, c1)] = act.astype(jnp.bfloat16)

        for j in range(n2):
            if first:
                w2_copy(j).wait()
            dst[start : start + count, pl.ds(j * c2, c2)] = jnp.dot(
                hidden[0:count, :], w2[j], preferred_element_type=jnp.float32
            ).astype(jnp.bfloat16)

    experts(buf, ret, 0, cap, True)

    for k in range(1, n):
        s1_copy(k).wait()
    stat2[me_dp] = sum(stat1[i] for i in range(n))
    for k in range(1, n_dp):
        s2_copy(k).start()

    for c in range(chunks):
        for k in range(1, n):
            out_copy(c, k).wait_recv()
        experts(recv, res, cap + c * span, span, False)
        for k in reversed(range(1, n)):
            back_copy(c, k).start()

    label_columns = to_columns(label.astype(jnp.float32))
    gate_column = to_columns(gate)[:, 0:1]

    def gather(start, count, first=0, length=n_tok):
        lanes = lax.broadcasted_iota(jnp.int32, (length, count), 1) + start
        wanted = label_columns[first : first + length, 0:1]
        one_hot = jnp.where(lanes.astype(jnp.float32) == wanted, 1.0, 0.0)
        return jnp.dot(
            one_hot.astype(jnp.bfloat16), ret[start : start + count, :],
            preferred_element_type=jnp.float32,
        )

    chosen[...] = gather(0, cap)

    for k in range(1, n_dp):
        s2_copy(k).wait()
    totals = jnp.transpose(sum(stat2[i] for i in range(n_dp)))
    denom = jnp.maximum(totals[0:2, n_exp : n_exp + 1], 1.0)
    mean = totals[0:2, 0:n_exp] / denom
    importance[...] = mean
    logs = jnp.log(jnp.where(mean == 0.0, 1.0, mean))
    entropies[:, 0:1] = totals[0:2, n_exp + 1 : n_exp + 2] / denom
    entropies[:, 1:2] = -jnp.sum(mean * logs, axis=1, keepdims=True)

    stores = [
        pltpu.make_async_copy(importance, importance_hbm, out_sem.at[0]),
        pltpu.make_async_copy(entropies, entropies_hbm, out_sem.at[1]),
    ]
    for store in stores:
        store.start()

    for c in range(chunks):
        for k in range(1, n):
            back_copy(c, k).wait_recv()
        if c < chunks - 1:
            chosen[...] += gather(cap + c * span, span)
    half = n_tok // 2
    for i in range(2):
        rows = pl.ds(i * half, half)
        last = gather(cap + (chunks - 1) * span, span, i * half, half)
        mixed[rows, :] = (
            gate_column[i * half : (i + 1) * half] * (chosen[rows, :] + last)
        ).astype(jnp.bfloat16)
        stores.append(
            pltpu.make_async_copy(mixed.at[rows], mixed_hbm.at[rows], out_sem.at[2 + i])
        )
        stores[-1].start()
    for store in stores:
        store.wait()

    for c in range(chunks):
        for k in range(1, n):
            out_copy(c, k).wait_send()
            back_copy(c, k).wait_send()


def write_out(*refs):
    sems, count = refs[-1], (len(refs) - 1) // 2
    copies = [pltpu.make_async_copy(refs[i], refs[count + i], sems.at[i]) for i in range(count)]
    for copy in copies:
        copy.start()
    for copy in copies:
        copy.wait()


def per_device(n, n_dp, tokens, router, w_in, w_out, assign, modality, slot):
    n_tok, width = tokens.shape
    n_exp = router.shape[1]
    ff = w_in.shape[2]
    cap = -(-(3 * n_tok // (2 * n_exp)) // 16) * 16
    chunks = 2 if cap % 32 == 0 else 1
    rows = n * cap
    c1, c2 = min(ff, 512), min(width, 256)
    stat_rows = -(-(n_exp + 2) // 8) * 8
    hbm = pl.BlockSpec(memory_space=pltpu.HBM)
    dma = pltpu.SemaphoreType.DMA
    block = pltpu.VMEM((rows, width), jnp.bfloat16)
    out_shape = (
        jax.ShapeDtypeStruct((n_tok, width), jnp.bfloat16),
        jax.ShapeDtypeStruct((2, n_exp), jnp.float32),
        jax.ShapeDtypeStruct((2, 2), jnp.float32),
    )
    results = pl.pallas_call(
        functools.partial(kernel, n, n_dp, cap, chunks),
        out_shape=out_shape,
        in_specs=[hbm] * 7,
        out_specs=(hbm, hbm, hbm),
        scratch_shapes=[
            *[pltpu.VMEM(out.shape, out.dtype) for out in out_shape],
            pltpu.VMEM((n_tok, width), jnp.bfloat16),
            pltpu.VMEM((n_exp, width), jnp.bfloat16),
            pltpu.VMEM((1, n_tok), jnp.int32),
            pltpu.VMEM((1, n_tok), jnp.int32),
            pltpu.VMEM((1, n_tok), jnp.int32),
            pltpu.VMEM((ff // c1, width, c1), jnp.bfloat16),
            pltpu.VMEM((width // c2, ff, c2), jnp.bfloat16),
            block, block, block, block,
            pltpu.VMEM((max(cap, rows - cap), ff), jnp.bfloat16),
            pltpu.VMEM((n_tok, width), jnp.float32),
            pltpu.VMEM((n, stat_rows, 128), jnp.float32),
            pltpu.VMEM((n_dp, stat_rows, 128), jnp.float32),
            dma((5,)), dma((4,)), dma((ff // c1,)), dma((width // c2,)),
            dma((chunks, n)), dma((chunks, n)), dma((chunks, n)), dma((chunks, n)),
            dma((n,)), dma((n,)), dma((n_dp,)), dma((n_dp,)),
        ],
        compiler_params=pltpu.CompilerParams(
            collective_id=0, has_side_effects=True, vmem_limit_bytes=VMEM_LIMIT
        ),
        cost_estimate=pl.CostEstimate(
            flops=4 * rows * width * ff, bytes_accessed=4 * width * ff, transcendentals=rows * ff
        ),
    )(
        tokens, router.T, w_in, w_out,
        assign.reshape(1, n_tok), modality.reshape(1, n_tok), slot.reshape(1, n_tok),
    )
    return pl.pallas_call(
        write_out, out_shape=out_shape, in_specs=[hbm] * 3, out_specs=(hbm,) * 3,
        scratch_shapes=[dma((3,))],
        compiler_params=pltpu.CompilerParams(vmem_limit_bytes=VMEM_LIMIT),
    )(*results)


def solution(mesh):
    return jax.shard_map(
        functools.partial(per_device, mesh.shape["expert"], mesh.shape["dp"]),
        mesh=mesh,
        in_specs=(
            P(("dp", "expert"), None),
            P(),
            P("expert", None, None),
            P("expert", None, None),
            P(("dp", "expert")),
            P(("dp", "expert")),
            P(("dp", "expert")),
        ),
        out_specs=(P(("dp", "expert"), None), P(), P()),
        check_vma=False,
    )
```

```python
import functools

import jax
import jax.numpy as jnp
from jax import lax
from jax.experimental import pallas as pl
from jax.experimental.pallas import tpu as pltpu
from jax.sharding import PartitionSpec as P

MESH = pl.DeviceIdType.MESH
VMEM_LIMIT = 63 * 2**20


def partner(me, k, n):
    out, bit = 0, 1
    while bit < n:
        digit = lax.rem(lax.div(me, bit), 2)
        if k & bit:
            digit = 1 - digit
        out = out + digit * bit
        bit *= 2
    return out


def to_columns(row):
    return jnp.transpose(jnp.broadcast_to(row, (128, row.shape[1])))


def kernel(
    n, n_dp, cap, chunks,
    tokens_hbm, router_hbm, w_in_hbm, w_out_hbm, assign_hbm, modality_hbm, slot_hbm,
    ret, take_hbm, gates_hbm, importance_hbm, entropies_hbm,
    take, gates, importance, entropies, tokens, router_t, assign, modality, slot, w1, w2, buf, recv, res, hidden, stat1, stat2,
    in_sem, out_sem, w1_sem, w2_sem, out_send, out_recv, back_send, back_recv, s1_send, s1_recv, s2_send, s2_recv,
):
    me = lax.axis_index("expert")
    me_dp = lax.axis_index("dp")
    peers = [partner(me, k, n) for k in range(n)]
    peers_dp = [partner(me_dp, k, n_dp) for k in range(n_dp)]
    n_tok, width = tokens.shape
    n_exp = router_t.shape[0]
    part = cap // chunks
    span = (n - 1) * part

    pairs = (
        (assign_hbm, assign), (slot_hbm, slot), (tokens_hbm, tokens),
        (router_hbm, router_t), (modality_hbm, modality),
    )
    loads = [pltpu.make_async_copy(a, b, in_sem.at[i]) for i, (a, b) in enumerate(pairs)]
    for load in loads:
        load.start()
    barrier = pltpu.get_barrier_semaphore()
    for k in range(1, n):
        pl.semaphore_signal(barrier, inc=1, device_id={"expert": peers[k]}, device_id_type=MESH)
    for k in range(1, n_dp):
        pl.semaphore_signal(barrier, inc=1, device_id={"dp": peers_dp[k]}, device_id_type=MESH)

    n1, n2 = w1.shape[0], w2.shape[0]
    c1, c2 = w1.shape[2], w2.shape[2]

    def w1_copy(j):
        return pltpu.make_async_copy(w_in_hbm.at[0, :, pl.ds(j * c1, c1)], w1.at[j], w1_sem.at[j])

    def w2_copy(j):
        return pltpu.make_async_copy(w_out_hbm.at[0, :, pl.ds(j * c2, c2)], w2.at[j], w2_sem.at[j])

    loads[0].wait()
    loads[1].wait()
    rel = jnp.bitwise_xor(assign[...], me)
    where_slot = slot[...]
    piece = lax.div(where_slot, part)
    label = jnp.where(
        rel == 0, where_slot, cap + piece * span + (rel - 1) * part + where_slot - piece * part
    )

    def place(dst, start, count):
        rows = lax.broadcasted_iota(jnp.int32, (count, n_tok), 0) + start
        one_hot = jnp.where(rows == label, 1.0, 0.0).astype(jnp.bfloat16)
        dst[start : start + count, :] = jnp.dot(
            one_hot, tokens[...], preferred_element_type=jnp.float32
        ).astype(jnp.bfloat16)

    def rows_of(c, k):
        return pl.ds(cap + c * span + (k - 1) * part, part)

    def send(src, dst, sems, c, k):
        rows = rows_of(c, k)
        return pltpu.make_async_remote_copy(
            src_ref=src.at[rows], dst_ref=dst.at[rows],
            send_sem=sems[0].at[c, k], recv_sem=sems[1].at[c, k],
            device_id={"expert": peers[k]}, device_id_type=MESH,
        )

    def out_copy(c, k):
        return send(buf, recv, (out_send, out_recv), c, k)

    def back_copy(c, k):
        return send(res, ret, (back_send, back_recv), c, k)

    loads[2].wait()
    for j in range(n1):
        w1_copy(j).start()
    for j in range(n2):
        w2_copy(j).start()
    for c in range(chunks):
        place(buf, cap + c * span, span)
        if c == 0:
            pl.semaphore_wait(barrier, n - 1 + n_dp - 1)
        for k in reversed(range(1, n)):
            out_copy(c, k).start()
    place(recv, 0, cap)

    loads[3].wait()
    loads[4].wait()
    logits = lax.dot_general(
        router_t[...], tokens[...], (((1,), (1,)), ((), ())), preferred_element_type=jnp.float32
    )
    shifted = logits - jnp.max(logits, axis=0, keepdims=True)
    unnorm = jnp.exp(shifted)
    total = jnp.sum(unnorm, axis=0, keepdims=True)
    probs = unnorm / total
    logp = shifted - jnp.log(total)
    picked = lax.broadcasted_iota(jnp.int32, probs.shape, 0) == assign[...]
    gate = jnp.sum(jnp.where(picked, probs, 0.0), axis=0, keepdims=True)
    entropy = -jnp.sum(probs * logp, axis=0, keepdims=True)
    kinds = [(modality[...] == m).astype(jnp.float32) for m in range(2)]

    def by_kind(values):
        first, second = (jnp.sum(values * kind, axis=1, keepdims=True) for kind in kinds)
        lane = lax.broadcasted_iota(jnp.int32, (values.shape[0], 128), 1)
        return jnp.where(lane == 0, first, jnp.where(lane == 1, second, 0.0))

    stat1[me] = jnp.zeros(stat1.shape[1:], jnp.float32)
    stat1[me, 0:n_exp, :] = by_kind(probs)
    stat1[me, n_exp : n_exp + 1, :] = by_kind(jnp.ones_like(gate))
    stat1[me, n_exp + 1 : n_exp + 2, :] = by_kind(entropy)

    def s1_copy(k):
        return pltpu.make_async_remote_copy(
            src_ref=stat1.at[me], dst_ref=stat1.at[me], send_sem=s1_send.at[k],
            recv_sem=s1_recv.at[k], device_id={"expert": peers[k]}, device_id_type=MESH,
        )

    def s2_copy(k):
        return pltpu.make_async_remote_copy(
            src_ref=stat2.at[me_dp], dst_ref=stat2.at[me_dp], send_sem=s2_send.at[k],
            recv_sem=s2_recv.at[k], device_id={"dp": peers_dp[k]}, device_id_type=MESH,
        )

    for k in range(1, n):
        s1_copy(k).start()

    def experts(start, count, first):
        for j in range(n1):
            if first:
                w1_copy(j).wait()
            act = jax.nn.gelu(
                jnp.dot(recv[start : start + count, :], w1[j], preferred_element_type=jnp.float32)
            )
            hidden[0:count, pl.ds(j * c1, c1)] = act.astype(jnp.bfloat16)
        for j in range(n2):
            if first:
                w2_copy(j).wait()
            res[start : start + count, pl.ds(j * c2, c2)] = jnp.dot(
                hidden[0:count, :], w2[j], preferred_element_type=jnp.float32
            ).astype(jnp.bfloat16)

    wanted = to_columns(label.astype(jnp.float32))[:, 0:1]
    lanes = lax.broadcasted_iota(jnp.int32, take.shape, 1).astype(jnp.float32)
    take[...] = jnp.where(lanes == wanted, 1.0, 0.0).astype(jnp.bfloat16)
    gates[...] = to_columns(gate)
    stores = [
        pltpu.make_async_copy(take, take_hbm, out_sem.at[0]),
        pltpu.make_async_copy(gates, gates_hbm, out_sem.at[1]),
    ]
    for store in stores:
        store.start()

    def first_sums():
        for k in range(1, n):
            s1_copy(k).wait()
        stat2[me_dp] = sum(stat1[i] for i in range(n))
        for k in range(1, n_dp):
            s2_copy(k).start()

    for c in range(chunks):
        for k in range(1, n):
            out_copy(c, k).wait_recv()
        if c == 0:
            experts(0, cap + span, True)
        else:
            experts(cap + c * span, span, False)
        for k in reversed(range(1, n)):
            back_copy(c, k).start()
        if c == 0:
            stores.append(
                pltpu.make_async_copy(res.at[pl.ds(0, cap)], ret.at[pl.ds(0, cap)], out_sem.at[2])
            )
            stores[-1].start()
            first_sums()

    for k in range(1, n_dp):
        s2_copy(k).wait()
    totals = jnp.transpose(sum(stat2[i] for i in range(n_dp)))
    denom = jnp.maximum(totals[0:2, n_exp : n_exp + 1], 1.0)
    mean = totals[0:2, 0:n_exp] / denom
    importance[...] = mean
    logs = jnp.log(jnp.where(mean == 0.0, 1.0, mean))
    entropies[:, 0:1] = totals[0:2, n_exp + 1 : n_exp + 2] / denom
    entropies[:, 1:2] = -jnp.sum(mean * logs, axis=1, keepdims=True)
    stores.append(pltpu.make_async_copy(importance, importance_hbm, out_sem.at[3]))
    stores.append(pltpu.make_async_copy(entropies, entropies_hbm, out_sem.at[4]))
    for store in stores[-2:]:
        store.start()

    for c in range(chunks):
        for k in range(1, n):
            out_copy(c, k).wait_send()
            back_copy(c, k).wait()
    for store in stores:
        store.wait()


def combine(
    ret_hbm, take_hbm, gates_hbm, importance_in, entropies_in,
    mixed_hbm, importance_hbm, entropies_hbm,
    ret, take, gates, importance, entropies, mixed, in_sem, out_sem,
):
    blocks, _, step = ret.shape
    small = (
        (take_hbm, take, None), (gates_hbm, gates, None),
        (importance_in, importance, importance_hbm), (entropies_in, entropies, entropies_hbm),
    )
    loads = [pltpu.make_async_copy(a, b, in_sem.at[i]) for i, (a, b, _) in enumerate(small)]
    columns = [pl.ds(j * step, step) for j in range(blocks)]
    pieces = [
        pltpu.make_async_copy(ret_hbm.at[:, columns[j]], ret.at[j], in_sem.at[len(small) + j])
        for j in range(blocks)
    ]
    for load in [*loads[:2], *pieces, *loads[2:]]:
        load.start()
    loads[0].wait()
    loads[1].wait()
    stores = []
    for j in range(blocks):
        pieces[j].wait()
        rows = jnp.dot(take[...], ret[j], preferred_element_type=jnp.float32)
        mixed[j] = (gates[:, 0:1] * rows).astype(jnp.bfloat16)
        stores.append(
            pltpu.make_async_copy(mixed.at[j], mixed_hbm.at[:, columns[j]], out_sem.at[j])
        )
        stores[-1].start()
    for i in (2, 3):
        loads[i].wait()
        stores.append(
            pltpu.make_async_copy(small[i][1], small[i][2], out_sem.at[blocks + i - 2])
        )
        stores[-1].start()
    for store in stores:
        store.wait()


def per_device(n, n_dp, tokens, router, w_in, w_out, assign, modality, slot):
    n_tok, width = tokens.shape
    n_exp = router.shape[1]
    ff = w_in.shape[2]
    cap = -(-(3 * n_tok // (2 * n_exp)) // 16) * 16
    chunks = 2 if cap % 32 == 0 else 1
    rows = n * cap
    c1, c2 = min(ff, 512), min(width, 256)
    stat_rows = -(-(n_exp + 2) // 8) * 8
    hbm = pl.BlockSpec(memory_space=pltpu.HBM)
    dma = pltpu.SemaphoreType.DMA
    block = pltpu.VMEM((rows, width), jnp.bfloat16)
    f32, bf16 = jnp.float32, jnp.bfloat16
    stats_shape = [jax.ShapeDtypeStruct((2, n_exp), f32), jax.ShapeDtypeStruct((2, 2), f32)]
    mixed_shape = jax.ShapeDtypeStruct((n_tok, width), bf16)
    carried = [
        jax.ShapeDtypeStruct((rows, width), bf16),
        jax.ShapeDtypeStruct((n_tok, rows), bf16),
        jax.ShapeDtypeStruct((n_tok, 128), f32),
        *stats_shape,
    ]
    results = pl.pallas_call(
        functools.partial(kernel, n, n_dp, cap, chunks),
        out_shape=carried,
        in_specs=[hbm] * 7,
        out_specs=[hbm] * 5,
        scratch_shapes=[
            *[pltpu.VMEM(out.shape, out.dtype) for out in carried[1:]],
            pltpu.VMEM((n_tok, width), jnp.bfloat16),
            pltpu.VMEM((n_exp, width), jnp.bfloat16),
            pltpu.VMEM((1, n_tok), jnp.int32),
            pltpu.VMEM((1, n_tok), jnp.int32),
            pltpu.VMEM((1, n_tok), jnp.int32),
            pltpu.VMEM((ff // c1, width, c1), jnp.bfloat16),
            pltpu.VMEM((width // c2, ff, c2), jnp.bfloat16),
            block, block, block,
            pltpu.VMEM((rows, ff), jnp.bfloat16),
            pltpu.VMEM((n, stat_rows, 128), jnp.float32),
            pltpu.VMEM((n_dp, stat_rows, 128), jnp.float32),
            dma((5,)), dma((5,)), dma((ff // c1,)), dma((width // c2,)),
            dma((chunks, n)), dma((chunks, n)), dma((chunks, n)), dma((chunks, n)),
            dma((n,)), dma((n,)), dma((n_dp,)), dma((n_dp,)),
        ],
        compiler_params=pltpu.CompilerParams(
            collective_id=0, has_side_effects=True, vmem_limit_bytes=VMEM_LIMIT
        ),
        cost_estimate=pl.CostEstimate(
            flops=4 * rows * width * ff, bytes_accessed=4 * width * ff, transcendentals=rows * ff
        ),
    )(
        tokens, router.T, w_in, w_out,
        assign.reshape(1, n_tok), modality.reshape(1, n_tok), slot.reshape(1, n_tok),
    )
    blocks = width // c2
    return pl.pallas_call(
        combine,
        out_shape=[mixed_shape, *stats_shape],
        in_specs=[hbm] * 5,
        out_specs=[hbm] * 3,
        scratch_shapes=[
            pltpu.VMEM((blocks, rows, c2), bf16),
            *[pltpu.VMEM(out.shape, out.dtype) for out in carried[1:]],
            pltpu.VMEM((blocks, n_tok, c2), bf16),
            dma((4 + blocks,)), dma((2 + blocks,)),
        ],
        compiler_params=pltpu.CompilerParams(vmem_limit_bytes=VMEM_LIMIT),
    )(*results)


def solution(mesh):
    return jax.shard_map(
        functools.partial(per_device, mesh.shape["expert"], mesh.shape["dp"]),
        mesh=mesh,
        in_specs=(
            P(("dp", "expert"), None),
            P(),
            P("expert", None, None),
            P("expert", None, None),
            P(("dp", "expert")),
            P(("dp", "expert")),
            P(("dp", "expert")),
        ),
        out_specs=(P(("dp", "expert"), None), P(), P()),
        check_vma=False,
    )
```

```python
import functools

import jax
import jax.numpy as jnp
from jax import lax
from jax.experimental import pallas as pl
from jax.experimental.pallas import tpu as pltpu
from jax.sharding import PartitionSpec as P

MESH = pl.DeviceIdType.MESH
VMEM_LIMIT = 63 * 2**20


def partner(me, k, n):
    out, bit = 0, 1
    while bit < n:
        digit = lax.rem(lax.div(me, bit), 2)
        if k & bit:
            digit = 1 - digit
        out = out + digit * bit
        bit *= 2
    return out


def to_columns(row):
    return jnp.transpose(jnp.broadcast_to(row, (128, row.shape[1])))


def kernel(
    n, n_dp, cap, chunks,
    tokens_hbm, router_hbm, w_in_hbm, w_out_hbm, assign_hbm, modality_hbm, slot_hbm,
    ret, take_hbm, gates_hbm, importance_hbm, entropies_hbm,
    take, gates, importance, entropies, tokens, router_t, assign, modality, slot, w1, w2, buf, recv, res, hidden, stat1, stat2,
    in_sem, out_sem, w1_sem, w2_sem, out_send, out_recv, back_send, back_recv, s1_send, s1_recv, s2_send, s2_recv,
):
    me = lax.axis_index("expert")
    me_dp = lax.axis_index("dp")
    peers = [partner(me, k, n) for k in range(n)]
    peers_dp = [partner(me_dp, k, n_dp) for k in range(n_dp)]
    n_tok, width = tokens.shape
    n_exp = router_t.shape[0]
    part = cap // chunks
    span = (n - 1) * part

    pairs = (
        (assign_hbm, assign), (slot_hbm, slot), (tokens_hbm, tokens),
        (router_hbm, router_t), (modality_hbm, modality),
    )
    loads = [pltpu.make_async_copy(a, b, in_sem.at[i]) for i, (a, b) in enumerate(pairs)]
    for load in loads:
        load.start()
    barrier = pltpu.get_barrier_semaphore()
    for k in range(1, n):
        pl.semaphore_signal(barrier, inc=1, device_id={"expert": peers[k]}, device_id_type=MESH)
    for k in range(1, n_dp):
        pl.semaphore_signal(barrier, inc=1, device_id={"dp": peers_dp[k]}, device_id_type=MESH)

    n1, n2 = w1.shape[0], w2.shape[0]
    c1, c2 = w1.shape[2], w2.shape[2]

    def w1_copy(j):
        return pltpu.make_async_copy(w_in_hbm.at[0, :, pl.ds(j * c1, c1)], w1.at[j], w1_sem.at[j])

    def w2_copy(j):
        return pltpu.make_async_copy(w_out_hbm.at[0, :, pl.ds(j * c2, c2)], w2.at[j], w2_sem.at[j])

    loads[0].wait()
    loads[1].wait()
    rel = jnp.bitwise_xor(assign[...], me)
    where_slot = slot[...]
    piece = lax.div(where_slot, part)
    label = jnp.where(
        rel == 0, where_slot, cap + piece * span + (rel - 1) * part + where_slot - piece * part
    )

    def place(dst, start, count):
        rows = lax.broadcasted_iota(jnp.int32, (count, n_tok), 0) + start
        one_hot = jnp.where(rows == label, 1.0, 0.0).astype(jnp.bfloat16)
        dst[start : start + count, :] = jnp.dot(
            one_hot, tokens[...], preferred_element_type=jnp.float32
        ).astype(jnp.bfloat16)

    def rows_of(c, k):
        return pl.ds(cap + c * span + (k - 1) * part, part)

    def send(src, dst, sems, c, k):
        rows = rows_of(c, k)
        return pltpu.make_async_remote_copy(
            src_ref=src.at[rows], dst_ref=dst.at[rows],
            send_sem=sems[0].at[c, k], recv_sem=sems[1].at[c, k],
            device_id={"expert": peers[k]}, device_id_type=MESH,
        )

    def out_copy(c, k):
        return send(buf, recv, (out_send, out_recv), c, k)

    def back_copy(c, k):
        return send(res, ret, (back_send, back_recv), c, k)

    loads[2].wait()
    for j in range(n1):
        w1_copy(j).start()
    for j in range(n2):
        w2_copy(j).start()
    for c in range(chunks):
        place(buf, cap + c * span, span)
        if c == 0:
            pl.semaphore_wait(barrier, n - 1 + n_dp - 1)
        for k in reversed(range(1, n)):
            out_copy(c, k).start()
    place(recv, 0, cap)

    loads[3].wait()
    loads[4].wait()
    logits = lax.dot_general(
        router_t[...], tokens[...], (((1,), (1,)), ((), ())), preferred_element_type=jnp.float32
    )
    shifted = logits - jnp.max(logits, axis=0, keepdims=True)
    unnorm = jnp.exp(shifted)
    total = jnp.sum(unnorm, axis=0, keepdims=True)
    probs = unnorm / total
    logp = shifted - jnp.log(total)
    picked = lax.broadcasted_iota(jnp.int32, probs.shape, 0) == assign[...]
    gate = jnp.sum(jnp.where(picked, probs, 0.0), axis=0, keepdims=True)
    entropy = -jnp.sum(probs * logp, axis=0, keepdims=True)
    kinds = [(modality[...] == m).astype(jnp.float32) for m in range(2)]

    def by_kind(values):
        first, second = (jnp.sum(values * kind, axis=1, keepdims=True) for kind in kinds)
        lane = lax.broadcasted_iota(jnp.int32, (values.shape[0], 128), 1)
        return jnp.where(lane == 0, first, jnp.where(lane == 1, second, 0.0))

    stat1[me] = jnp.zeros(stat1.shape[1:], jnp.float32)
    stat1[me, 0:n_exp, :] = by_kind(probs)
    stat1[me, n_exp : n_exp + 1, :] = by_kind(jnp.ones_like(gate))
    stat1[me, n_exp + 1 : n_exp + 2, :] = by_kind(entropy)

    def s1_copy(k):
        return pltpu.make_async_remote_copy(
            src_ref=stat1.at[me], dst_ref=stat1.at[me], send_sem=s1_send.at[k],
            recv_sem=s1_recv.at[k], device_id={"expert": peers[k]}, device_id_type=MESH,
        )

    def s2_copy(k):
        return pltpu.make_async_remote_copy(
            src_ref=stat2.at[me_dp], dst_ref=stat2.at[me_dp], send_sem=s2_send.at[k],
            recv_sem=s2_recv.at[k], device_id={"dp": peers_dp[k]}, device_id_type=MESH,
        )

    for k in range(1, n):
        s1_copy(k).start()

    def experts(start, count, first):
        for j in range(n1):
            if first:
                w1_copy(j).wait()
            act = jax.nn.gelu(
                jnp.dot(recv[start : start + count, :], w1[j], preferred_element_type=jnp.float32)
            )
            hidden[0:count, pl.ds(j * c1, c1)] = act.astype(jnp.bfloat16)
        for j in range(n2):
            if first:
                w2_copy(j).wait()
            res[start : start + count, pl.ds(j * c2, c2)] = jnp.dot(
                hidden[0:count, :], w2[j], preferred_element_type=jnp.float32
            ).astype(jnp.bfloat16)

    wanted = to_columns(label.astype(jnp.float32))[:, 0:1]
    lanes = lax.broadcasted_iota(jnp.int32, take.shape, 1).astype(jnp.float32)
    take[...] = jnp.where(lanes == wanted, 1.0, 0.0).astype(jnp.bfloat16)
    gates[...] = to_columns(gate)
    stores = [
        pltpu.make_async_copy(take, take_hbm, out_sem.at[0]),
        pltpu.make_async_copy(gates, gates_hbm, out_sem.at[1]),
    ]
    for store in stores:
        store.start()

    def first_sums():
        for k in range(1, n):
            s1_copy(k).wait()
        stat2[me_dp] = sum(stat1[i] for i in range(n))
        for k in range(1, n_dp):
            s2_copy(k).start()

    for c in range(chunks):
        for k in range(1, n):
            out_copy(c, k).wait_recv()
        if c == 0:
            experts(0, cap + span, True)
        else:
            experts(cap + c * span, span, False)
        for k in reversed(range(1, n)):
            back_copy(c, k).start()
        if c == 0:
            stores.append(
                pltpu.make_async_copy(res.at[pl.ds(0, cap)], ret.at[pl.ds(0, cap)], out_sem.at[2])
            )
            stores[-1].start()
            first_sums()

    for k in range(1, n_dp):
        s2_copy(k).wait()
    totals = jnp.transpose(sum(stat2[i] for i in range(n_dp)))
    denom = jnp.maximum(totals[0:2, n_exp : n_exp + 1], 1.0)
    mean = totals[0:2, 0:n_exp] / denom
    importance[...] = mean
    logs = jnp.log(jnp.where(mean == 0.0, 1.0, mean))
    entropies[:, 0:1] = totals[0:2, n_exp + 1 : n_exp + 2] / denom
    entropies[:, 1:2] = -jnp.sum(mean * logs, axis=1, keepdims=True)
    stores.append(pltpu.make_async_copy(importance, importance_hbm, out_sem.at[3]))
    stores.append(pltpu.make_async_copy(entropies, entropies_hbm, out_sem.at[4]))
    for store in stores[-2:]:
        store.start()

    for c in range(chunks):
        for k in range(1, n):
            out_copy(c, k).wait_send()
            back_copy(c, k).wait()
    for store in stores:
        store.wait()


def combine(
    ret_hbm, take_hbm, gates_hbm, importance_in, entropies_in,
    mixed_hbm, importance_hbm, entropies_hbm,
    ret, take, gates, importance, entropies, mixed, in_sem, out_sem,
):
    blocks, _, step = ret.shape
    small = (
        (take_hbm, take, None), (gates_hbm, gates, None),
        (importance_in, importance, importance_hbm), (entropies_in, entropies, entropies_hbm),
    )
    loads = [pltpu.make_async_copy(a, b, in_sem.at[i]) for i, (a, b, _) in enumerate(small)]
    columns = [pl.ds(j * step, step) for j in range(blocks)]
    pieces = [
        pltpu.make_async_copy(ret_hbm.at[:, columns[j]], ret.at[j], in_sem.at[len(small) + j])
        for j in range(blocks)
    ]
    for load in [*loads[:2], *pieces, *loads[2:]]:
        load.start()
    loads[0].wait()
    loads[1].wait()
    stores = []
    for j in range(blocks):
        pieces[j].wait()
        rows = jnp.dot(take[...], ret[j], preferred_element_type=jnp.float32)
        mixed[j] = (gates[:, 0:1] * rows).astype(jnp.bfloat16)
        stores.append(
            pltpu.make_async_copy(mixed.at[j], mixed_hbm.at[:, columns[j]], out_sem.at[j])
        )
        stores[-1].start()
    for i in (2, 3):
        loads[i].wait()
        stores.append(
            pltpu.make_async_copy(small[i][1], small[i][2], out_sem.at[blocks + i - 2])
        )
        stores[-1].start()
    for store in stores:
        store.wait()


def per_device(n, n_dp, tokens, router, w_in, w_out, assign, modality, slot):
    n_tok, width = tokens.shape
    n_exp = router.shape[1]
    ff = w_in.shape[2]
    cap = -(-(3 * n_tok // (2 * n_exp)) // 16) * 16
    chunks = next(c for c in (3, 2, 1) if cap % (16 * c) == 0)
    rows = n * cap
    c1, c2 = min(ff, 512), min(width, 256)
    stat_rows = -(-(n_exp + 2) // 8) * 8
    hbm = pl.BlockSpec(memory_space=pltpu.HBM)
    dma = pltpu.SemaphoreType.DMA
    block = pltpu.VMEM((rows, width), jnp.bfloat16)
    f32, bf16 = jnp.float32, jnp.bfloat16
    stats_shape = [jax.ShapeDtypeStruct((2, n_exp), f32), jax.ShapeDtypeStruct((2, 2), f32)]
    mixed_shape = jax.ShapeDtypeStruct((n_tok, width), bf16)
    carried = [
        jax.ShapeDtypeStruct((rows, width), bf16),
        jax.ShapeDtypeStruct((n_tok, rows), bf16),
        jax.ShapeDtypeStruct((n_tok, 128), f32),
        *stats_shape,
    ]
    results = pl.pallas_call(
        functools.partial(kernel, n, n_dp, cap, chunks),
        out_shape=carried,
        in_specs=[hbm] * 7,
        out_specs=[hbm] * 5,
        scratch_shapes=[
            *[pltpu.VMEM(out.shape, out.dtype) for out in carried[1:]],
            pltpu.VMEM((n_tok, width), jnp.bfloat16),
            pltpu.VMEM((n_exp, width), jnp.bfloat16),
            pltpu.VMEM((1, n_tok), jnp.int32),
            pltpu.VMEM((1, n_tok), jnp.int32),
            pltpu.VMEM((1, n_tok), jnp.int32),
            pltpu.VMEM((ff // c1, width, c1), jnp.bfloat16),
            pltpu.VMEM((width // c2, ff, c2), jnp.bfloat16),
            block, block, block,
            pltpu.VMEM((rows, ff), jnp.bfloat16),
            pltpu.VMEM((n, stat_rows, 128), jnp.float32),
            pltpu.VMEM((n_dp, stat_rows, 128), jnp.float32),
            dma((5,)), dma((5,)), dma((ff // c1,)), dma((width // c2,)),
            dma((chunks, n)), dma((chunks, n)), dma((chunks, n)), dma((chunks, n)),
            dma((n,)), dma((n,)), dma((n_dp,)), dma((n_dp,)),
        ],
        compiler_params=pltpu.CompilerParams(
            collective_id=0, has_side_effects=True, vmem_limit_bytes=VMEM_LIMIT
        ),
        cost_estimate=pl.CostEstimate(
            flops=4 * rows * width * ff, bytes_accessed=4 * width * ff, transcendentals=rows * ff
        ),
    )(
        tokens, router.T, w_in, w_out,
        assign.reshape(1, n_tok), modality.reshape(1, n_tok), slot.reshape(1, n_tok),
    )
    blocks = width // c2
    return pl.pallas_call(
        combine,
        out_shape=[mixed_shape, *stats_shape],
        in_specs=[hbm] * 5,
        out_specs=[hbm] * 3,
        scratch_shapes=[
            pltpu.VMEM((blocks, rows, c2), bf16),
            *[pltpu.VMEM(out.shape, out.dtype) for out in carried[1:]],
            pltpu.VMEM((blocks, n_tok, c2), bf16),
            dma((4 + blocks,)), dma((2 + blocks,)),
        ],
        compiler_params=pltpu.CompilerParams(vmem_limit_bytes=VMEM_LIMIT),
    )(*results)


def solution(mesh):
    return jax.shard_map(
        functools.partial(per_device, mesh.shape["expert"], mesh.shape["dp"]),
        mesh=mesh,
        in_specs=(
            P(("dp", "expert"), None),
            P(),
            P("expert", None, None),
            P("expert", None, None),
            P(("dp", "expert")),
            P(("dp", "expert")),
            P(("dp", "expert")),
        ),
        out_specs=(P(("dp", "expert"), None), P(), P()),
        check_vma=False,
    )
```

```python
import functools
import math

import jax
import jax.numpy as jnp
from jax import lax
from jax.experimental import pallas as pl
from jax.experimental.pallas import tpu as pltpu
from jax.sharding import PartitionSpec as P

MESH = pl.DeviceIdType.MESH
VMEM_LIMIT = 63 * 2**20


def partner(me, k, n):
    out, bit = 0, 1
    while bit < n:
        digit = lax.rem(lax.div(me, bit), 2)
        if k & bit:
            digit = 1 - digit
        out = out + digit * bit
        bit *= 2
    return out


def gelu(x):
    scale = math.sqrt(2.0 / math.pi)
    half = 0.5 * x
    return half + half * jnp.tanh(x * (scale + (scale * 0.044715) * (x * x)))


def to_columns(row):
    return jnp.transpose(jnp.broadcast_to(row, (128, row.shape[1])))


def kernel(
    n, n_dp, cap, chunks,
    tokens_hbm, router_hbm, w_in_hbm, w_out_hbm, assign_hbm, modality_hbm, slot_hbm,
    ret, take_hbm, gates_hbm, importance_hbm, entropies_hbm,
    take, gates, importance, entropies, tokens, router_t, assign, modality, slot, w1, w2, buf, recv, res, hidden, stat1, stat2, stat3,
    in_sem, out_sem, w1_sem, w2_sem, out_send, out_recv, back_send, back_recv, s1_send, s1_recv, s2_send, s2_recv,
    s3_send, s3_recv, entered,
):
    me = lax.axis_index("expert")
    me_dp = lax.axis_index("dp")
    peers = [partner(me, k, n) for k in range(n)]
    peers_dp = [partner(me_dp, k, n_dp) for k in range(n_dp)]
    n_tok, width = tokens.shape
    n_exp = router_t.shape[0]
    part = cap // chunks
    span = (n - 1) * part

    barrier = pltpu.get_barrier_semaphore()
    for k in range(1, n):
        @pl.when(me != k)
        def _():
            pl.semaphore_signal(
                barrier, inc=1, device_id={"expert": peers[k]}, device_id_type=MESH
            )

    @pl.when(me == 0)
    def _():
        for k in range(1, n_dp):
            pl.semaphore_signal(
                barrier, inc=1, device_id={"dp": peers_dp[k]}, device_id_type=MESH
            )

    pairs = (
        (assign_hbm, assign), (slot_hbm, slot), (tokens_hbm, tokens),
        (router_hbm, router_t), (modality_hbm, modality),
    )
    loads = [pltpu.make_async_copy(a, b, in_sem.at[i]) for i, (a, b) in enumerate(pairs)]
    for load in loads:
        load.start()

    def await_group():
        @pl.when(me != 0)
        def _():
            pl.semaphore_wait(barrier, n - 1)
            pl.semaphore_signal(entered, inc=1, device_id={"expert": 0}, device_id_type=MESH)

        @pl.when(me == 0)
        def _():
            pl.semaphore_wait(entered, n - 1)

    n1, n2 = w1.shape[0], w2.shape[0]
    c1, c2 = w1.shape[2], w2.shape[2]

    def w1_copy(j):
        return pltpu.make_async_copy(w_in_hbm.at[0, :, pl.ds(j * c1, c1)], w1.at[j], w1_sem.at[j])

    def w2_copy(j):
        return pltpu.make_async_copy(w_out_hbm.at[0, :, pl.ds(j * c2, c2)], w2.at[j], w2_sem.at[j])

    loads[0].wait()
    loads[1].wait()
    rel = jnp.bitwise_xor(assign[...], me)
    where_slot = slot[...]
    piece = lax.div(where_slot, part)
    label = jnp.where(
        rel == 0, where_slot, cap + piece * span + (rel - 1) * part + where_slot - piece * part
    )

    def place(dst, start, count):
        rows = lax.broadcasted_iota(jnp.int32, (count, n_tok), 0) + start
        one_hot = jnp.where(rows == label, 1.0, 0.0).astype(jnp.bfloat16)
        dst[start : start + count, :] = jnp.dot(
            one_hot, tokens[...], preferred_element_type=jnp.float32
        ).astype(jnp.bfloat16)

    def rows_of(c, k):
        return pl.ds(cap + c * span + (k - 1) * part, part)

    def send(src, dst, sems, c, k):
        rows = rows_of(c, k)
        return pltpu.make_async_remote_copy(
            src_ref=src.at[rows], dst_ref=dst.at[rows],
            send_sem=sems[0].at[c, k], recv_sem=sems[1].at[c, k],
            device_id={"expert": peers[k]}, device_id_type=MESH,
        )

    def out_copy(c, k):
        return send(buf, recv, (out_send, out_recv), c, k)

    def back_copy(c, k):
        return send(res, ret, (back_send, back_recv), c, k)

    loads[2].wait()
    for j in range(n1):
        w1_copy(j).start()
    for j in range(n2):
        w2_copy(j).start()
    for c in range(chunks):
        place(buf, cap + c * span, span)
        if c == 0:
            await_group()
        for k in reversed(range(1, n)):
            out_copy(c, k).start()
    place(recv, 0, cap)

    loads[3].wait()
    loads[4].wait()
    logits = lax.dot_general(
        router_t[...], tokens[...], (((1,), (1,)), ((), ())), preferred_element_type=jnp.float32
    )
    shifted = logits - jnp.max(logits, axis=0, keepdims=True)
    unnorm = jnp.exp(shifted)
    total = jnp.sum(unnorm, axis=0, keepdims=True)
    probs = unnorm / total
    logp = shifted - jnp.log(total)
    picked = lax.broadcasted_iota(jnp.int32, probs.shape, 0) == assign[...]
    gate = jnp.sum(jnp.where(picked, probs, 0.0), axis=0, keepdims=True)
    entropy = -jnp.sum(probs * logp, axis=0, keepdims=True)
    kinds = [(modality[...] == m).astype(jnp.float32) for m in range(2)]

    def by_kind(values):
        first, second = (jnp.sum(values * kind, axis=1, keepdims=True) for kind in kinds)
        lane = lax.broadcasted_iota(jnp.int32, (values.shape[0], 128), 1)
        return jnp.where(lane == 0, first, jnp.where(lane == 1, second, 0.0))

    stat1[me] = jnp.zeros(stat1.shape[1:], jnp.float32)
    stat1[me, 0:n_exp, :] = by_kind(probs)
    stat1[me, n_exp : n_exp + 1, :] = by_kind(jnp.ones_like(gate))
    stat1[me, n_exp + 1 : n_exp + 2, :] = by_kind(entropy)

    def s1_copy(i):
        return pltpu.make_async_remote_copy(
            src_ref=stat1.at[i], dst_ref=stat1.at[i], send_sem=s1_send,
            recv_sem=s1_recv.at[i], device_id={"expert": 0}, device_id_type=MESH,
        )

    def s2_copy(k):
        return pltpu.make_async_remote_copy(
            src_ref=stat2.at[me_dp], dst_ref=stat2.at[me_dp], send_sem=s2_send.at[k],
            recv_sem=s2_recv.at[k], device_id={"dp": peers_dp[k]}, device_id_type=MESH,
        )

    def s3_copy(k):
        return pltpu.make_async_remote_copy(
            src_ref=stat3, dst_ref=stat3, send_sem=s3_send.at[k], recv_sem=s3_recv,
            device_id={"expert": k}, device_id_type=MESH,
        )

    @pl.when(me != 0)
    def _():
        s1_copy(me).start()

    def first_sums():
        @pl.when(me == 0)
        def _():
            for i in range(1, n):
                s1_copy(i).wait_recv()
            stat2[me_dp] = sum(stat1[i] for i in range(n))
            pl.semaphore_wait(barrier, n_dp - 1)
            for k in range(1, n_dp):
                s2_copy(k).start()

    def last_sums():
        @pl.when(me == 0)
        def _():
            for k in range(1, n_dp):
                s2_copy(k).wait()
            stat3[...] = sum(stat2[i] for i in range(n_dp))
            for k in range(1, n):
                s3_copy(k).start()
            for k in range(1, n):
                s3_copy(k).wait_send()

        @pl.when(me != 0)
        def _():
            s1_copy(me).wait_send()
            s3_copy(0).wait_recv()

    def experts(start, count, first):
        for j in range(n1):
            if first:
                w1_copy(j).wait()
            act = gelu(
                jnp.dot(recv[start : start + count, :], w1[j], preferred_element_type=jnp.float32)
            )
            hidden[0:count, pl.ds(j * c1, c1)] = act.astype(jnp.bfloat16)
        for j in range(n2):
            if first:
                w2_copy(j).wait()
            res[start : start + count, pl.ds(j * c2, c2)] = jnp.dot(
                hidden[0:count, :], w2[j], preferred_element_type=jnp.float32
            ).astype(jnp.bfloat16)

    wanted = to_columns(label.astype(jnp.float32))[:, 0:1]
    lanes = lax.broadcasted_iota(jnp.int32, take.shape, 1).astype(jnp.float32)
    take[...] = jnp.where(lanes == wanted, 1.0, 0.0).astype(jnp.bfloat16)
    gates[...] = to_columns(gate)
    stores = [
        pltpu.make_async_copy(take, take_hbm, out_sem.at[0]),
        pltpu.make_async_copy(gates, gates_hbm, out_sem.at[1]),
    ]
    for store in stores:
        store.start()

    for c in range(chunks):
        for k in range(1, n):
            out_copy(c, k).wait_recv()
        if c == 0:
            experts(0, cap + span, True)
        else:
            experts(cap + c * span, span, False)
        for k in reversed(range(1, n)):
            back_copy(c, k).start()
        if c == 0:
            stores.append(
                pltpu.make_async_copy(res.at[pl.ds(0, cap)], ret.at[pl.ds(0, cap)], out_sem.at[2])
            )
            stores[-1].start()
            first_sums()

    last_sums()
    totals = jnp.transpose(stat3[...])
    denom = jnp.maximum(totals[0:2, n_exp : n_exp + 1], 1.0)
    mean = totals[0:2, 0:n_exp] / denom
    importance[...] = mean
    logs = jnp.log(jnp.where(mean == 0.0, 1.0, mean))
    entropies[:, 0:1] = totals[0:2, n_exp + 1 : n_exp + 2] / denom
    entropies[:, 1:2] = -jnp.sum(mean * logs, axis=1, keepdims=True)
    stores.append(pltpu.make_async_copy(importance, importance_hbm, out_sem.at[3]))
    stores.append(pltpu.make_async_copy(entropies, entropies_hbm, out_sem.at[4]))
    for store in stores[-2:]:
        store.start()

    for c in range(chunks):
        for k in range(1, n):
            out_copy(c, k).wait_send()
            back_copy(c, k).wait()
    for store in stores:
        store.wait()


def combine(
    ret_hbm, take_hbm, gates_hbm, importance_in, entropies_in,
    mixed_hbm, importance_hbm, entropies_hbm,
    ret, take, gates, importance, entropies, mixed, in_sem, out_sem,
):
    blocks, _, step = ret.shape
    small = (
        (take_hbm, take, None), (gates_hbm, gates, None),
        (importance_in, importance, importance_hbm), (entropies_in, entropies, entropies_hbm),
    )
    loads = [pltpu.make_async_copy(a, b, in_sem.at[i]) for i, (a, b, _) in enumerate(small)]
    columns = [pl.ds(j * step, step) for j in range(blocks)]
    pieces = [
        pltpu.make_async_copy(ret_hbm.at[:, columns[j]], ret.at[j], in_sem.at[len(small) + j])
        for j in range(blocks)
    ]
    for load in [*loads[:2], *pieces, *loads[2:]]:
        load.start()
    loads[0].wait()
    loads[1].wait()
    stores = []
    for j in range(blocks):
        pieces[j].wait()
        rows = jnp.dot(take[...], ret[j], preferred_element_type=jnp.float32)
        mixed[j] = (gates[:, 0:1] * rows).astype(jnp.bfloat16)
        stores.append(
            pltpu.make_async_copy(mixed.at[j], mixed_hbm.at[:, columns[j]], out_sem.at[j])
        )
        stores[-1].start()
    for i in (2, 3):
        loads[i].wait()
        stores.append(
            pltpu.make_async_copy(small[i][1], small[i][2], out_sem.at[blocks + i - 2])
        )
        stores[-1].start()
    for store in stores:
        store.wait()


def per_device(n, n_dp, tokens, router, w_in, w_out, assign, modality, slot):
    n_tok, width = tokens.shape
    n_exp = router.shape[1]
    ff = w_in.shape[2]
    cap = -(-(3 * n_tok // (2 * n_exp)) // 16) * 16
    chunks = next(c for c in (3, 2, 1) if cap % (16 * c) == 0)
    rows = n * cap
    c1, c2 = min(ff, 512), min(width, 256)
    stat_rows = -(-(n_exp + 2) // 8) * 8
    hbm = pl.BlockSpec(memory_space=pltpu.HBM)
    dma = pltpu.SemaphoreType.DMA
    block = pltpu.VMEM((rows, width), jnp.bfloat16)
    f32, bf16 = jnp.float32, jnp.bfloat16
    stats_shape = [jax.ShapeDtypeStruct((2, n_exp), f32), jax.ShapeDtypeStruct((2, 2), f32)]
    mixed_shape = jax.ShapeDtypeStruct((n_tok, width), bf16)
    carried = [
        jax.ShapeDtypeStruct((rows, width), bf16),
        jax.ShapeDtypeStruct((n_tok, rows), bf16),
        jax.ShapeDtypeStruct((n_tok, 128), f32),
        *stats_shape,
    ]
    results = pl.pallas_call(
        functools.partial(kernel, n, n_dp, cap, chunks),
        out_shape=carried,
        in_specs=[hbm] * 7,
        out_specs=[hbm] * 5,
        scratch_shapes=[
            *[pltpu.VMEM(out.shape, out.dtype) for out in carried[1:]],
            pltpu.VMEM((n_tok, width), jnp.bfloat16),
            pltpu.VMEM((n_exp, width), jnp.bfloat16),
            pltpu.VMEM((1, n_tok), jnp.int32),
            pltpu.VMEM((1, n_tok), jnp.int32),
            pltpu.VMEM((1, n_tok), jnp.int32),
            pltpu.VMEM((ff // c1, width, c1), jnp.bfloat16),
            pltpu.VMEM((width // c2, ff, c2), jnp.bfloat16),
            block, block, block,
            pltpu.VMEM((rows, ff), jnp.bfloat16),
            pltpu.VMEM((n, stat_rows, 128), jnp.float32),
            pltpu.VMEM((n_dp, stat_rows, 128), jnp.float32),
            pltpu.VMEM((stat_rows, 128), jnp.float32),
            dma((5,)), dma((5,)), dma((ff // c1,)), dma((width // c2,)),
            dma((chunks, n)), dma((chunks, n)), dma((chunks, n)), dma((chunks, n)),
            dma, dma((n,)), dma((n_dp,)), dma((n_dp,)), dma((n,)), dma,
            pltpu.SemaphoreType.REGULAR,
        ],
        compiler_params=pltpu.CompilerParams(
            collective_id=0, has_side_effects=True, vmem_limit_bytes=VMEM_LIMIT
        ),
        cost_estimate=pl.CostEstimate(
            flops=4 * rows * width * ff, bytes_accessed=4 * width * ff, transcendentals=rows * ff
        ),
    )(
        tokens, router.T, w_in, w_out,
        assign.reshape(1, n_tok), modality.reshape(1, n_tok), slot.reshape(1, n_tok),
    )
    blocks = width // c2
    return pl.pallas_call(
        combine,
        out_shape=[mixed_shape, *stats_shape],
        in_specs=[hbm] * 5,
        out_specs=[hbm] * 3,
        scratch_shapes=[
            pltpu.VMEM((blocks, rows, c2), bf16),
            *[pltpu.VMEM(out.shape, out.dtype) for out in carried[1:]],
            pltpu.VMEM((blocks, n_tok, c2), bf16),
            dma((4 + blocks,)), dma((2 + blocks,)),
        ],
        compiler_params=pltpu.CompilerParams(vmem_limit_bytes=VMEM_LIMIT),
    )(*results)


def solution(mesh):
    return jax.shard_map(
        functools.partial(per_device, mesh.shape["expert"], mesh.shape["dp"]),
        mesh=mesh,
        in_specs=(
            P(("dp", "expert"), None),
            P(),
            P("expert", None, None),
            P("expert", None, None),
            P(("dp", "expert")),
            P(("dp", "expert")),
            P(("dp", "expert")),
        ),
        out_specs=(P(("dp", "expert"), None), P(), P()),
        check_vma=False,
    )
```

```python
import functools
import math

import jax
import jax.numpy as jnp
from jax import lax
from jax.experimental import pallas as pl
from jax.experimental.pallas import tpu as pltpu
from jax.sharding import PartitionSpec as P

MESH = pl.DeviceIdType.MESH
VMEM_LIMIT = 63 * 2**20


def partner(me, k, n):
    out, bit = 0, 1
    while bit < n:
        digit = lax.rem(lax.div(me, bit), 2)
        if k & bit:
            digit = 1 - digit
        out = out + digit * bit
        bit *= 2
    return out


def gelu(x):
    scale = math.sqrt(2.0 / math.pi)
    half = 0.5 * x
    return half + half * jnp.tanh(x * (scale + (scale * 0.044715) * (x * x)))


def to_columns(row):
    return jnp.transpose(jnp.broadcast_to(row, (128, row.shape[1])))


def kernel(
    n, n_dp, cap, chunks,
    tokens_hbm, router_hbm, w_in_hbm, w_out_hbm, assign_hbm, modality_hbm, slot_hbm,
    ret, picks_hbm, importance_hbm, entropies_hbm,
    picks, importance, entropies, tokens, router_t, assign, modality, slot, w1, w2, buf, recv, res, hidden, stat1, stat2, stat3,
    in_sem, out_sem, w1_sem, w2_sem, out_send, out_recv, back_send, back_recv, s1_send, s1_recv, s2_send, s2_recv,
    s3_send, s3_recv, entered,
):
    me = lax.axis_index("expert")
    me_dp = lax.axis_index("dp")
    lead = n - 1
    others = range(n - 1)
    peers = [partner(me, k, n) for k in range(n)]
    peers_dp = [partner(me_dp, k, n_dp) for k in range(n_dp)]
    n_tok, width = tokens.shape
    n_exp = router_t.shape[0]
    part = cap // chunks
    span = (n - 1) * part

    barrier = pltpu.get_barrier_semaphore()
    for k in range(1, n):
        @pl.when(me != lead ^ k)
        def _():
            pl.semaphore_signal(
                barrier, inc=1, device_id={"expert": peers[k]}, device_id_type=MESH
            )

    @pl.when(me == lead)
    def _():
        for k in range(1, n_dp):
            pl.semaphore_signal(
                barrier, inc=1, device_id={"dp": peers_dp[k]}, device_id_type=MESH
            )

    pairs = (
        (assign_hbm, assign), (slot_hbm, slot), (tokens_hbm, tokens),
        (router_hbm, router_t), (modality_hbm, modality),
    )
    loads = [pltpu.make_async_copy(a, b, in_sem.at[i]) for i, (a, b) in enumerate(pairs)]
    for load in loads:
        load.start()

    def await_group():
        @pl.when(me != lead)
        def _():
            pl.semaphore_wait(barrier, n - 1)
            pl.semaphore_signal(entered, inc=1, device_id={"expert": lead}, device_id_type=MESH)

        @pl.when(me == lead)
        def _():
            pl.semaphore_wait(entered, n - 1)

    n1, n2 = w1.shape[0], w2.shape[0]
    c1, c2 = w1.shape[2], w2.shape[2]

    def w1_copy(j):
        return pltpu.make_async_copy(w_in_hbm.at[0, :, pl.ds(j * c1, c1)], w1.at[j], w1_sem.at[j])

    def w2_copy(j):
        return pltpu.make_async_copy(w_out_hbm.at[0, :, pl.ds(j * c2, c2)], w2.at[j], w2_sem.at[j])

    loads[0].wait()
    loads[1].wait()
    rel = jnp.bitwise_xor(assign[...], me)
    where_slot = slot[...]
    piece = lax.div(where_slot, part)
    label = jnp.where(
        rel == 0, where_slot, cap + piece * span + (rel - 1) * part + where_slot - piece * part
    )

    def place(dst, start, count):
        rows = lax.broadcasted_iota(jnp.int32, (count, n_tok), 0) + start
        one_hot = jnp.where(rows == label, 1.0, 0.0).astype(jnp.bfloat16)
        dst[start : start + count, :] = jnp.dot(
            one_hot, tokens[...], preferred_element_type=jnp.float32
        ).astype(jnp.bfloat16)

    def rows_of(c, k):
        return pl.ds(cap + c * span + (k - 1) * part, part)

    def send(src, dst, sems, c, k):
        rows = rows_of(c, k)
        return pltpu.make_async_remote_copy(
            src_ref=src.at[rows], dst_ref=dst.at[rows],
            send_sem=sems[0].at[c, k], recv_sem=sems[1].at[c, k],
            device_id={"expert": peers[k]}, device_id_type=MESH,
        )

    def out_copy(c, k):
        return send(buf, recv, (out_send, out_recv), c, k)

    def back_copy(c, k):
        return send(res, ret, (back_send, back_recv), c, k)

    loads[2].wait()
    for j in range(n1):
        w1_copy(j).start()
    for j in range(n2):
        w2_copy(j).start()
    for c in range(chunks):
        place(buf, cap + c * span, span)
        if c == 0:
            await_group()
        for k in reversed(range(1, n)):
            out_copy(c, k).start()
    place(recv, 0, cap)

    loads[3].wait()
    loads[4].wait()
    logits = lax.dot_general(
        router_t[...], tokens[...], (((1,), (1,)), ((), ())), preferred_element_type=jnp.float32
    )
    shifted = logits - jnp.max(logits, axis=0, keepdims=True)
    unnorm = jnp.exp(shifted)
    total = jnp.sum(unnorm, axis=0, keepdims=True)
    probs = unnorm / total
    logp = shifted - jnp.log(total)
    picked = lax.broadcasted_iota(jnp.int32, probs.shape, 0) == assign[...]
    gate = jnp.sum(jnp.where(picked, probs, 0.0), axis=0, keepdims=True)
    entropy = -jnp.sum(probs * logp, axis=0, keepdims=True)
    kinds = [(modality[...] == m).astype(jnp.float32) for m in range(2)]

    def by_kind(values):
        first, second = (jnp.sum(values * kind, axis=1, keepdims=True) for kind in kinds)
        lane = lax.broadcasted_iota(jnp.int32, (values.shape[0], 128), 1)
        return jnp.where(lane == 0, first, jnp.where(lane == 1, second, 0.0))

    stat1[me] = jnp.zeros(stat1.shape[1:], jnp.float32)
    stat1[me, 0:n_exp, :] = by_kind(probs)
    stat1[me, n_exp : n_exp + 1, :] = by_kind(jnp.ones_like(gate))
    stat1[me, n_exp + 1 : n_exp + 2, :] = by_kind(entropy)

    def s1_copy(i):
        return pltpu.make_async_remote_copy(
            src_ref=stat1.at[i], dst_ref=stat1.at[i], send_sem=s1_send,
            recv_sem=s1_recv.at[i], device_id={"expert": lead}, device_id_type=MESH,
        )

    def s2_copy(k):
        return pltpu.make_async_remote_copy(
            src_ref=stat2.at[me_dp], dst_ref=stat2.at[me_dp], send_sem=s2_send.at[k],
            recv_sem=s2_recv.at[k], device_id={"dp": peers_dp[k]}, device_id_type=MESH,
        )

    def s3_copy(k):
        return pltpu.make_async_remote_copy(
            src_ref=stat3, dst_ref=stat3, send_sem=s3_send.at[k], recv_sem=s3_recv,
            device_id={"expert": k}, device_id_type=MESH,
        )

    @pl.when(me != lead)
    def _():
        s1_copy(me).start()

    def first_sums():
        @pl.when(me == lead)
        def _():
            for i in others:
                s1_copy(i).wait_recv()
            stat2[me_dp] = sum(stat1[i] for i in range(n))
            pl.semaphore_wait(barrier, n_dp - 1)
            for k in range(1, n_dp):
                s2_copy(k).start()

    def last_sums():
        @pl.when(me == lead)
        def _():
            for k in range(1, n_dp):
                s2_copy(k).wait()
            stat3[...] = sum(stat2[i] for i in range(n_dp))
            for k in others:
                s3_copy(k).start()
            for k in others:
                s3_copy(k).wait_send()

        @pl.when(me != lead)
        def _():
            s1_copy(me).wait_send()
            s3_copy(0).wait_recv()

    def experts(start, count, first):
        for j in range(n1):
            if first:
                w1_copy(j).wait()
            act = gelu(
                jnp.dot(recv[start : start + count, :], w1[j], preferred_element_type=jnp.float32)
            )
            hidden[0:count, pl.ds(j * c1, c1)] = act.astype(jnp.bfloat16)
        for j in range(n2):
            if first:
                w2_copy(j).wait()
            res[start : start + count, pl.ds(j * c2, c2)] = jnp.dot(
                hidden[0:count, :], w2[j], preferred_element_type=jnp.float32
            ).astype(jnp.bfloat16)

    lanes = lax.broadcasted_iota(jnp.int32, picks.shape, 1)
    picks[...] = jnp.where(lanes == 0, to_columns(label.astype(jnp.float32)), to_columns(gate))
    stores = [pltpu.make_async_copy(picks, picks_hbm, out_sem.at[0])]
    for store in stores:
        store.start()

    for c in range(chunks):
        for k in range(1, n):
            out_copy(c, k).wait_recv()
        if c == 0:
            experts(0, cap + span, True)
        else:
            experts(cap + c * span, span, False)
        for k in reversed(range(1, n)):
            back_copy(c, k).start()
        if c == 0:
            stores.append(
                pltpu.make_async_copy(res.at[pl.ds(0, cap)], ret.at[pl.ds(0, cap)], out_sem.at[1])
            )
            stores[-1].start()
            first_sums()

    last_sums()
    totals = jnp.transpose(stat3[...])
    denom = jnp.maximum(totals[0:2, n_exp : n_exp + 1], 1.0)
    mean = totals[0:2, 0:n_exp] / denom
    importance[...] = mean
    logs = jnp.log(jnp.where(mean == 0.0, 1.0, mean))
    entropies[:, 0:1] = totals[0:2, n_exp + 1 : n_exp + 2] / denom
    entropies[:, 1:2] = -jnp.sum(mean * logs, axis=1, keepdims=True)
    stores.append(pltpu.make_async_copy(importance, importance_hbm, out_sem.at[2]))
    stores.append(pltpu.make_async_copy(entropies, entropies_hbm, out_sem.at[3]))
    for store in stores[-2:]:
        store.start()

    for c in range(chunks):
        for k in range(1, n):
            out_copy(c, k).wait_send()
            back_copy(c, k).wait()
    for store in stores:
        store.wait()


def combine(
    ret_hbm, picks_hbm, importance_in, entropies_in, mixed_hbm, importance_hbm, entropies_hbm,
    ret, picks, importance, entropies, mixed, in_sem, out_sem,
):
    blocks, n_rows, step = ret.shape
    columns = [pl.ds(j * step, step) for j in range(blocks)]
    pairs = (
        (picks_hbm, picks), (importance_in, importance), (entropies_in, entropies),
        *((ret_hbm.at[:, columns[j]], ret.at[j]) for j in range(blocks)),
    )
    loads = [pltpu.make_async_copy(a, b, in_sem.at[i]) for i, (a, b) in enumerate(pairs)]
    pairs = (
        (importance, importance_hbm), (entropies, entropies_hbm),
        *((mixed.at[j], mixed_hbm.at[:, columns[j]]) for j in range(blocks)),
    )
    stores = [pltpu.make_async_copy(a, b, out_sem.at[i]) for i, (a, b) in enumerate(pairs)]
    for load in loads:
        load.start()
    for i in range(3):
        loads[i].wait()
    for i in range(2):
        stores[i].start()
    lanes = lax.broadcasted_iota(jnp.int32, (picks.shape[0], n_rows), 1).astype(jnp.float32)
    take = jnp.where(lanes == picks[:, 0:1], 1.0, 0.0).astype(jnp.bfloat16)
    for j in range(blocks):
        loads[3 + j].wait()
        rows = jnp.dot(take, ret[j], preferred_element_type=jnp.float32)
        mixed[j] = (picks[:, 1:2] * rows).astype(jnp.bfloat16)
        stores[2 + j].start()
    for store in stores:
        store.wait()


def per_device(n, n_dp, tokens, router, w_in, w_out, assign, modality, slot):
    n_tok, width = tokens.shape
    n_exp = router.shape[1]
    ff = w_in.shape[2]
    cap = -(-(3 * n_tok // (2 * n_exp)) // 16) * 16
    chunks = next(c for c in (3, 2, 1) if cap % (16 * c) == 0)
    rows = n * cap
    c1, c2 = min(ff, 256), min(width, 256)
    stat_rows = -(-(n_exp + 2) // 8) * 8
    hbm = pl.BlockSpec(memory_space=pltpu.HBM)
    dma = pltpu.SemaphoreType.DMA
    block = pltpu.VMEM((rows, width), jnp.bfloat16)
    f32, bf16 = jnp.float32, jnp.bfloat16
    stats_shape = [jax.ShapeDtypeStruct((2, n_exp), f32), jax.ShapeDtypeStruct((2, 2), f32)]
    mixed_shape = jax.ShapeDtypeStruct((n_tok, width), bf16)
    carried = [
        jax.ShapeDtypeStruct((rows, width), bf16),
        jax.ShapeDtypeStruct((n_tok, 128), f32),
        *stats_shape,
    ]
    results = pl.pallas_call(
        functools.partial(kernel, n, n_dp, cap, chunks),
        out_shape=carried,
        in_specs=[hbm] * 7,
        out_specs=[hbm] * 4,
        scratch_shapes=[
            *[pltpu.VMEM(out.shape, out.dtype) for out in carried[1:]],
            pltpu.VMEM((n_tok, width), jnp.bfloat16),
            pltpu.VMEM((n_exp, width), jnp.bfloat16),
            pltpu.VMEM((1, n_tok), jnp.int32),
            pltpu.VMEM((1, n_tok), jnp.int32),
            pltpu.VMEM((1, n_tok), jnp.int32),
            pltpu.VMEM((ff // c1, width, c1), jnp.bfloat16),
            pltpu.VMEM((width // c2, ff, c2), jnp.bfloat16),
            block, block, block,
            pltpu.VMEM((rows, ff), jnp.bfloat16),
            pltpu.VMEM((n, stat_rows, 128), jnp.float32),
            pltpu.VMEM((n_dp, stat_rows, 128), jnp.float32),
            pltpu.VMEM((stat_rows, 128), jnp.float32),
            dma((5,)), dma((4,)), dma((ff // c1,)), dma((width // c2,)),
            dma((chunks, n)), dma((chunks, n)), dma((chunks, n)), dma((chunks, n)),
            dma, dma((n,)), dma((n_dp,)), dma((n_dp,)), dma((n,)), dma,
            pltpu.SemaphoreType.REGULAR,
        ],
        compiler_params=pltpu.CompilerParams(
            collective_id=0, has_side_effects=True, vmem_limit_bytes=VMEM_LIMIT
        ),
        cost_estimate=pl.CostEstimate(
            flops=4 * rows * width * ff, bytes_accessed=4 * width * ff, transcendentals=rows * ff
        ),
    )(
        tokens, router.T, w_in, w_out,
        assign.reshape(1, n_tok), modality.reshape(1, n_tok), slot.reshape(1, n_tok),
    )
    blocks = width // c2
    return pl.pallas_call(
        combine,
        out_shape=[mixed_shape, *stats_shape],
        in_specs=[hbm] * 4,
        out_specs=[hbm] * 3,
        scratch_shapes=[
            pltpu.VMEM((blocks, rows, c2), bf16),
            *[pltpu.VMEM(out.shape, out.dtype) for out in carried[1:]],
            pltpu.VMEM((blocks, n_tok, c2), bf16),
            dma((3 + blocks,)), dma((2 + blocks,)),
        ],
        compiler_params=pltpu.CompilerParams(vmem_limit_bytes=VMEM_LIMIT),
    )(*results)


def solution(mesh):
    return jax.shard_map(
        functools.partial(per_device, mesh.shape["expert"], mesh.shape["dp"]),
        mesh=mesh,
        in_specs=(
            P(("dp", "expert"), None),
            P(),
            P("expert", None, None),
            P("expert", None, None),
            P(("dp", "expert")),
            P(("dp", "expert")),
            P(("dp", "expert")),
        ),
        out_specs=(P(("dp", "expert"), None), P(), P()),
        check_vma=False,
    )
```

```python
import functools
import math

import jax
import jax.numpy as jnp
from jax import lax
from jax.experimental import pallas as pl
from jax.experimental.pallas import tpu as pltpu
from jax.sharding import PartitionSpec as P

MESH = pl.DeviceIdType.MESH
VMEM_LIMIT = 63 * 2**20


def partner(me, k, n):
    out, bit = 0, 1
    while bit < n:
        digit = lax.rem(lax.div(me, bit), 2)
        if k & bit:
            digit = 1 - digit
        out = out + digit * bit
        bit *= 2
    return out


def gelu(x):
    scale = math.sqrt(2.0 / math.pi)
    half = 0.5 * x
    return half + half * jnp.tanh(x * (scale + (scale * 0.044715) * (x * x)))


def to_columns(row):
    return jnp.transpose(jnp.broadcast_to(row, (128, row.shape[1])))


def kernel(
    n, n_dp, cap, parts,
    tokens_hbm, router_hbm, w_in_hbm, w_out_hbm, assign_hbm, modality_hbm, slot_hbm,
    ret, picks_hbm, importance_hbm, entropies_hbm,
    picks, importance, entropies, tokens, router_t, assign, modality, slot, w1, w2, buf, recv, res, hidden, stat1, stat2, stat3,
    in_sem, out_sem, w1_sem, w2_sem, out_send, out_recv, back_send, back_recv, s1_send, s1_recv, s2_send, s2_recv,
    s3_send, s3_recv, entered,
):
    me = lax.axis_index("expert")
    me_dp = lax.axis_index("dp")
    lead = 0
    others = range(1, n)
    peers = [partner(me, k, n) for k in range(n)]
    peers_dp = [partner(me_dp, k, n_dp) for k in range(n_dp)]
    n_tok, width = tokens.shape
    n_exp = router_t.shape[0]
    starts = [sum(parts[:c]) for c in range(len(parts))]
    bases = [cap + (n - 1) * start for start in starts]
    spans = [(n - 1) * part for part in parts]
    chunks = len(parts)

    barrier = pltpu.get_barrier_semaphore()
    for k in range(1, n):
        @pl.when(me != lead ^ k)
        def _():
            pl.semaphore_signal(
                barrier, inc=1, device_id={"expert": peers[k]}, device_id_type=MESH
            )

    @pl.when(me == lead)
    def _():
        for k in range(1, n_dp):
            pl.semaphore_signal(
                barrier, inc=1, device_id={"dp": peers_dp[k]}, device_id_type=MESH
            )

    pairs = (
        (assign_hbm, assign), (slot_hbm, slot), (tokens_hbm, tokens),
        (router_hbm, router_t), (modality_hbm, modality),
    )
    loads = [pltpu.make_async_copy(a, b, in_sem.at[i]) for i, (a, b) in enumerate(pairs)]
    for load in loads:
        load.start()

    def greet_group():
        @pl.when(me != lead)
        def _():
            pl.semaphore_wait(barrier, n - 1)
            pl.semaphore_signal(
                entered.at[me], inc=1, device_id={"expert": lead}, device_id_type=MESH
            )

    def await_member(k):
        @pl.when(me == lead)
        def _():
            pl.semaphore_wait(entered.at[k], 1)

    n1, n2 = w1.shape[0], w2.shape[0]
    c1, c2 = w1.shape[2], w2.shape[2]

    def w1_copy(j):
        return pltpu.make_async_copy(w_in_hbm.at[0, :, pl.ds(j * c1, c1)], w1.at[j], w1_sem.at[j])

    def w2_copy(j):
        return pltpu.make_async_copy(w_out_hbm.at[0, :, pl.ds(j * c2, c2)], w2.at[j], w2_sem.at[j])

    loads[0].wait()
    loads[1].wait()
    rel = jnp.bitwise_xor(assign[...], me)
    where_slot = slot[...]
    label = where_slot
    for start, base, part in zip(starts, bases, parts):
        inside = jnp.logical_and(rel > 0, where_slot >= start)
        label = jnp.where(inside, base + (rel - 1) * part + where_slot - start, label)

    def place(dst, start, count):
        rows = lax.broadcasted_iota(jnp.int32, (count, n_tok), 0) + start
        one_hot = jnp.where(rows == label, 1.0, 0.0).astype(jnp.bfloat16)
        dst[start : start + count, :] = jnp.dot(
            one_hot, tokens[...], preferred_element_type=jnp.float32
        ).astype(jnp.bfloat16)

    def rows_of(c, k):
        return pl.ds(bases[c] + (k - 1) * parts[c], parts[c])

    def send(src, dst, sems, c, k):
        rows = rows_of(c, k)
        return pltpu.make_async_remote_copy(
            src_ref=src.at[rows], dst_ref=dst.at[rows],
            send_sem=sems[0].at[c, k], recv_sem=sems[1].at[c, k],
            device_id={"expert": peers[k]}, device_id_type=MESH,
        )

    def out_copy(c, k):
        return send(buf, recv, (out_send, out_recv), c, k)

    def back_copy(c, k):
        return send(res, ret, (back_send, back_recv), c, k)

    loads[2].wait()
    for j in range(n1):
        w1_copy(j).start()
    for j in range(n2):
        w2_copy(j).start()
    for c in range(chunks):
        place(buf, bases[c], spans[c])
        if c == 0:
            greet_group()
        for k in reversed(range(1, n)):
            if c == 0:
                await_member(k)
            out_copy(c, k).start()
    place(recv, 0, cap)

    loads[3].wait()
    loads[4].wait()
    logits = lax.dot_general(
        router_t[...], tokens[...], (((1,), (1,)), ((), ())), preferred_element_type=jnp.float32
    )
    shifted = logits - jnp.max(logits, axis=0, keepdims=True)
    unnorm = jnp.exp(shifted)
    total = jnp.sum(unnorm, axis=0, keepdims=True)
    probs = unnorm / total
    logp = shifted - jnp.log(total)
    picked = lax.broadcasted_iota(jnp.int32, probs.shape, 0) == assign[...]
    gate = jnp.sum(jnp.where(picked, probs, 0.0), axis=0, keepdims=True)
    entropy = -jnp.sum(probs * logp, axis=0, keepdims=True)
    kinds = [(modality[...] == m).astype(jnp.float32) for m in range(2)]

    def by_kind(values):
        first, second = (jnp.sum(values * kind, axis=1, keepdims=True) for kind in kinds)
        lane = lax.broadcasted_iota(jnp.int32, (values.shape[0], 128), 1)
        return jnp.where(lane == 0, first, jnp.where(lane == 1, second, 0.0))

    stat1[me] = jnp.zeros(stat1.shape[1:], jnp.float32)
    stat1[me, 0:n_exp, :] = by_kind(probs)
    stat1[me, n_exp : n_exp + 1, :] = by_kind(jnp.ones_like(gate))
    stat1[me, n_exp + 1 : n_exp + 2, :] = by_kind(entropy)

    def s1_copy(i):
        return pltpu.make_async_remote_copy(
            src_ref=stat1.at[i], dst_ref=stat1.at[i], send_sem=s1_send,
            recv_sem=s1_recv.at[i], device_id={"expert": lead}, device_id_type=MESH,
        )

    def s2_copy(k):
        return pltpu.make_async_remote_copy(
            src_ref=stat2.at[me_dp], dst_ref=stat2.at[me_dp], send_sem=s2_send.at[k],
            recv_sem=s2_recv.at[k], device_id={"dp": peers_dp[k]}, device_id_type=MESH,
        )

    def s3_copy(k):
        return pltpu.make_async_remote_copy(
            src_ref=stat3, dst_ref=stat3, send_sem=s3_send.at[k], recv_sem=s3_recv,
            device_id={"expert": k}, device_id_type=MESH,
        )

    @pl.when(me != lead)
    def _():
        s1_copy(me).start()

    def first_sums():
        @pl.when(me == lead)
        def _():
            for i in others:
                s1_copy(i).wait_recv()
            stat2[me_dp] = sum(stat1[i] for i in range(n))
            pl.semaphore_wait(barrier, n_dp - 1)
            for k in range(1, n_dp):
                s2_copy(k).start()

    def last_sums():
        @pl.when(me == lead)
        def _():
            for k in range(1, n_dp):
                s2_copy(k).wait()
            stat3[...] = sum(stat2[i] for i in range(n_dp))
            for k in others:
                s3_copy(k).start()
            for k in others:
                s3_copy(k).wait_send()

        @pl.when(me != lead)
        def _():
            s1_copy(me).wait_send()
            s3_copy(0).wait_recv()

    def experts(start, count, first):
        for j in range(n1):
            if first:
                w1_copy(j).wait()
            act = gelu(
                jnp.dot(recv[start : start + count, :], w1[j], preferred_element_type=jnp.float32)
            )
            hidden[0:count, pl.ds(j * c1, c1)] = act.astype(jnp.bfloat16)
        for j in range(n2):
            if first:
                w2_copy(j).wait()
            res[start : start + count, pl.ds(j * c2, c2)] = jnp.dot(
                hidden[0:count, :], w2[j], preferred_element_type=jnp.float32
            ).astype(jnp.bfloat16)

    lanes = lax.broadcasted_iota(jnp.int32, picks.shape, 1)
    picks[...] = jnp.where(lanes == 0, to_columns(label.astype(jnp.float32)), to_columns(gate))
    stores = [pltpu.make_async_copy(picks, picks_hbm, out_sem.at[0])]
    for store in stores:
        store.start()

    for c in range(chunks):
        for k in range(1, n):
            out_copy(c, k).wait_recv()
        if c == 0:
            experts(0, cap + spans[c], True)
        else:
            experts(bases[c], spans[c], False)
        for k in reversed(range(1, n)):
            back_copy(c, k).start()
        if c == 0:
            stores.append(
                pltpu.make_async_copy(res.at[pl.ds(0, cap)], ret.at[pl.ds(0, cap)], out_sem.at[1])
            )
            stores[-1].start()
            first_sums()

    last_sums()
    totals = jnp.transpose(stat3[...])
    denom = jnp.maximum(totals[0:2, n_exp : n_exp + 1], 1.0)
    mean = totals[0:2, 0:n_exp] / denom
    importance[...] = mean
    logs = jnp.log(jnp.where(mean == 0.0, 1.0, mean))
    entropies[:, 0:1] = totals[0:2, n_exp + 1 : n_exp + 2] / denom
    entropies[:, 1:2] = -jnp.sum(mean * logs, axis=1, keepdims=True)
    stores.append(pltpu.make_async_copy(importance, importance_hbm, out_sem.at[2]))
    stores.append(pltpu.make_async_copy(entropies, entropies_hbm, out_sem.at[3]))
    for store in stores[-2:]:
        store.start()

    for c in range(chunks):
        for k in range(1, n):
            out_copy(c, k).wait_send()
            back_copy(c, k).wait()
    for store in stores:
        store.wait()


def combine(
    ret_hbm, picks_hbm, importance_in, entropies_in, mixed_hbm, importance_hbm, entropies_hbm,
    ret, picks, importance, entropies, mixed, in_sem, out_sem,
):
    blocks, n_rows, step = ret.shape
    columns = [pl.ds(j * step, step) for j in range(blocks)]
    pairs = (
        (picks_hbm, picks), (importance_in, importance), (entropies_in, entropies),
        *((ret_hbm.at[:, columns[j]], ret.at[j]) for j in range(blocks)),
    )
    loads = [pltpu.make_async_copy(a, b, in_sem.at[i]) for i, (a, b) in enumerate(pairs)]
    pairs = (
        (importance, importance_hbm), (entropies, entropies_hbm),
        *((mixed.at[j], mixed_hbm.at[:, columns[j]]) for j in range(blocks)),
    )
    stores = [pltpu.make_async_copy(a, b, out_sem.at[i]) for i, (a, b) in enumerate(pairs)]
    for load in loads:
        load.start()
    for i in range(3):
        loads[i].wait()
    for i in range(2):
        stores[i].start()
    lanes = lax.broadcasted_iota(jnp.int32, (picks.shape[0], n_rows), 1).astype(jnp.float32)
    take = jnp.where(lanes == picks[:, 0:1], 1.0, 0.0).astype(jnp.bfloat16)
    for j in range(blocks):
        loads[3 + j].wait()
        rows = jnp.dot(take, ret[j], preferred_element_type=jnp.float32)
        mixed[j] = (picks[:, 1:2] * rows).astype(jnp.bfloat16)
        stores[2 + j].start()
    for store in stores:
        store.wait()


def per_device(n, n_dp, tokens, router, w_in, w_out, assign, modality, slot):
    n_tok, width = tokens.shape
    n_exp = router.shape[1]
    ff = w_in.shape[2]
    cap = -(-(3 * n_tok // (2 * n_exp)) // 16) * 16
    units = cap // 16
    parts = [16 * size for size in (1, units - 1 - units // 3, units // 3) if size]
    chunks = len(parts)
    rows = n * cap
    c1, c2 = min(ff, 512), min(width, 256)
    stat_rows = -(-(n_exp + 2) // 8) * 8
    hbm = pl.BlockSpec(memory_space=pltpu.HBM)
    dma = pltpu.SemaphoreType.DMA
    block = pltpu.VMEM((rows, width), jnp.bfloat16)
    f32, bf16 = jnp.float32, jnp.bfloat16
    stats_shape = [jax.ShapeDtypeStruct((2, n_exp), f32), jax.ShapeDtypeStruct((2, 2), f32)]
    mixed_shape = jax.ShapeDtypeStruct((n_tok, width), bf16)
    carried = [
        jax.ShapeDtypeStruct((rows, width), bf16),
        jax.ShapeDtypeStruct((n_tok, 128), f32),
        *stats_shape,
    ]
    results = pl.pallas_call(
        functools.partial(kernel, n, n_dp, cap, parts),
        out_shape=carried,
        in_specs=[hbm] * 7,
        out_specs=[hbm] * 4,
        scratch_shapes=[
            *[pltpu.VMEM(out.shape, out.dtype) for out in carried[1:]],
            pltpu.VMEM((n_tok, width), jnp.bfloat16),
            pltpu.VMEM((n_exp, width), jnp.bfloat16),
            pltpu.VMEM((1, n_tok), jnp.int32),
            pltpu.VMEM((1, n_tok), jnp.int32),
            pltpu.VMEM((1, n_tok), jnp.int32),
            pltpu.VMEM((ff // c1, width, c1), jnp.bfloat16),
            pltpu.VMEM((width // c2, ff, c2), jnp.bfloat16),
            block, block, block,
            pltpu.VMEM((rows, ff), jnp.bfloat16),
            pltpu.VMEM((n, stat_rows, 128), jnp.float32),
            pltpu.VMEM((n_dp, stat_rows, 128), jnp.float32),
            pltpu.VMEM((stat_rows, 128), jnp.float32),
            dma((5,)), dma((4,)), dma((ff // c1,)), dma((width // c2,)),
            dma((chunks, n)), dma((chunks, n)), dma((chunks, n)), dma((chunks, n)),
            dma, dma((n,)), dma((n_dp,)), dma((n_dp,)), dma((n,)), dma,
            pltpu.SemaphoreType.REGULAR((n,)),
        ],
        compiler_params=pltpu.CompilerParams(
            collective_id=0, has_side_effects=True, vmem_limit_bytes=VMEM_LIMIT
        ),
        cost_estimate=pl.CostEstimate(
            flops=4 * rows * width * ff, bytes_accessed=4 * width * ff, transcendentals=rows * ff
        ),
    )(
        tokens, router.T, w_in, w_out,
        assign.reshape(1, n_tok), modality.reshape(1, n_tok), slot.reshape(1, n_tok),
    )
    blocks = width // c2
    return pl.pallas_call(
        combine,
        out_shape=[mixed_shape, *stats_shape],
        in_specs=[hbm] * 4,
        out_specs=[hbm] * 3,
        scratch_shapes=[
            pltpu.VMEM((blocks, rows, c2), bf16),
            *[pltpu.VMEM(out.shape, out.dtype) for out in carried[1:]],
            pltpu.VMEM((blocks, n_tok, c2), bf16),
            dma((3 + blocks,)), dma((2 + blocks,)),
        ],
        compiler_params=pltpu.CompilerParams(vmem_limit_bytes=VMEM_LIMIT),
    )(*results)


def solution(mesh):
    return jax.shard_map(
        functools.partial(per_device, mesh.shape["expert"], mesh.shape["dp"]),
        mesh=mesh,
        in_specs=(
            P(("dp", "expert"), None),
            P(),
            P("expert", None, None),
            P("expert", None, None),
            P(("dp", "expert")),
            P(("dp", "expert")),
            P(("dp", "expert")),
        ),
        out_specs=(P(("dp", "expert"), None), P(), P()),
        check_vma=False,
    )
```

```python
import functools
import math

import jax
import jax.numpy as jnp
from jax import lax
from jax.experimental import pallas as pl
from jax.experimental.pallas import tpu as pltpu
from jax.sharding import PartitionSpec as P

MESH = pl.DeviceIdType.MESH
VMEM_LIMIT = 63 * 2**20


def partner(me, k, n):
    out, bit = 0, 1
    while bit < n:
        digit = lax.rem(lax.div(me, bit), 2)
        if k & bit:
            digit = 1 - digit
        out = out + digit * bit
        bit *= 2
    return out


def gelu(x):
    scale = math.sqrt(2.0 / math.pi)
    half = 0.5 * x
    return half + half * jnp.tanh(x * (scale + (scale * 0.044715) * (x * x)))


def to_columns(row):
    return jnp.transpose(jnp.broadcast_to(row, (128, row.shape[1])))


def kernel(
    n, n_dp, cap, parts,
    tokens_hbm, router_hbm, w_in_hbm, w_out_hbm, assign_hbm, modality_hbm, slot_hbm,
    ret, picks_hbm, importance_hbm, entropies_hbm,
    picks, importance, entropies, tokens, router_t, assign, modality, slot, w1, w2, buf, recv, res, hidden, stat1, stat2, stat3,
    in_sem, out_sem, w1_sem, w2_sem, out_send, out_recv, back_send, back_recv, s1_send, s1_recv, s2_send, s2_recv,
    s3_send, s3_recv, entered,
):
    me = lax.axis_index("expert")
    me_dp = lax.axis_index("dp")
    lead = 0
    others = range(1, n)
    peers = [partner(me, k, n) for k in range(n)]
    peers_dp = [partner(me_dp, k, n_dp) for k in range(n_dp)]
    n_tok, width = tokens.shape
    n_exp = router_t.shape[0]
    starts = [sum(parts[:c]) for c in range(len(parts))]
    bases = [cap + (n - 1) * start for start in starts]
    spans = [(n - 1) * part for part in parts]
    chunks = len(parts)

    barrier = pltpu.get_barrier_semaphore()
    for k in range(1, n):
        @pl.when(me != lead ^ k)
        def _():
            pl.semaphore_signal(
                barrier, inc=1, device_id={"expert": peers[k]}, device_id_type=MESH
            )

    @pl.when(me == lead)
    def _():
        for k in range(1, n_dp):
            pl.semaphore_signal(
                barrier, inc=1, device_id={"dp": peers_dp[k]}, device_id_type=MESH
            )

    pairs = (
        (assign_hbm, assign), (slot_hbm, slot), (tokens_hbm, tokens),
        (router_hbm, router_t), (modality_hbm, modality),
    )
    loads = [pltpu.make_async_copy(a, b, in_sem.at[i]) for i, (a, b) in enumerate(pairs)]
    for load in loads:
        load.start()

    def greet_group():
        @pl.when(me != lead)
        def _():
            pl.semaphore_wait(barrier, n - 1)
            pl.semaphore_signal(
                entered.at[me], inc=1, device_id={"expert": lead}, device_id_type=MESH
            )

    def await_member(k):
        @pl.when(me == lead)
        def _():
            pl.semaphore_wait(entered.at[k], 1)

    n1, n2 = w1.shape[0], w2.shape[0]
    c1, c2 = w1.shape[2], w2.shape[2]

    def w1_copy(j):
        return pltpu.make_async_copy(w_in_hbm.at[0, :, pl.ds(j * c1, c1)], w1.at[j], w1_sem.at[j])

    def w2_copy(j):
        return pltpu.make_async_copy(w_out_hbm.at[0, :, pl.ds(j * c2, c2)], w2.at[j], w2_sem.at[j])

    loads[0].wait()
    loads[1].wait()
    rel = jnp.bitwise_xor(assign[...], me)
    where_slot = slot[...]
    label = where_slot
    for start, base, part in zip(starts, bases, parts):
        inside = jnp.logical_and(rel > 0, where_slot >= start)
        label = jnp.where(inside, base + (rel - 1) * part + where_slot - start, label)

    def place(dst, start, count):
        rows = lax.broadcasted_iota(jnp.int32, (count, n_tok), 0) + start
        one_hot = jnp.where(rows == label, 1.0, 0.0).astype(jnp.bfloat16)
        dst[start : start + count, :] = jnp.dot(
            one_hot, tokens[...], preferred_element_type=jnp.float32
        ).astype(jnp.bfloat16)

    def rows_of(c, k):
        return pl.ds(bases[c] + (k - 1) * parts[c], parts[c])

    def send(src, dst, sems, c, k):
        rows = rows_of(c, k)
        return pltpu.make_async_remote_copy(
            src_ref=src.at[rows], dst_ref=dst.at[rows],
            send_sem=sems[0].at[c, k], recv_sem=sems[1].at[c, k],
            device_id={"expert": peers[k]}, device_id_type=MESH,
        )

    def out_copy(c, k):
        return send(buf, recv, (out_send, out_recv), c, k)

    def back_copy(c, k):
        return send(res, ret, (back_send, back_recv), c, k)

    orders = ([n - 1, *range(1, n - 1)], list(reversed(range(1, n))))

    def start_all(copy, c):
        for parity, order in enumerate(orders):
            @pl.when(lax.rem(me_dp, 2) == parity)
            def _():
                for k in order:
                    copy(c, k).start()

    loads[2].wait()
    for j in range(n1):
        w1_copy(j).start()
    for j in range(n2):
        w2_copy(j).start()
    for c in range(chunks):
        place(buf, bases[c], spans[c])
        if c == 0:
            greet_group()
            for k in reversed(range(1, n)):
                await_member(k)
        start_all(out_copy, c)
    place(recv, 0, cap)

    loads[3].wait()
    loads[4].wait()
    logits = lax.dot_general(
        router_t[...], tokens[...], (((1,), (1,)), ((), ())), preferred_element_type=jnp.float32
    )
    shifted = logits - jnp.max(logits, axis=0, keepdims=True)
    unnorm = jnp.exp(shifted)
    total = jnp.sum(unnorm, axis=0, keepdims=True)
    probs = unnorm / total
    logp = shifted - jnp.log(total)
    picked = lax.broadcasted_iota(jnp.int32, probs.shape, 0) == assign[...]
    gate = jnp.sum(jnp.where(picked, probs, 0.0), axis=0, keepdims=True)
    entropy = -jnp.sum(probs * logp, axis=0, keepdims=True)
    kinds = [(modality[...] == m).astype(jnp.float32) for m in range(2)]

    def by_kind(values):
        first, second = (jnp.sum(values * kind, axis=1, keepdims=True) for kind in kinds)
        lane = lax.broadcasted_iota(jnp.int32, (values.shape[0], 128), 1)
        return jnp.where(lane == 0, first, jnp.where(lane == 1, second, 0.0))

    stat1[me] = jnp.zeros(stat1.shape[1:], jnp.float32)
    stat1[me, 0:n_exp, :] = by_kind(probs)
    stat1[me, n_exp : n_exp + 1, :] = by_kind(jnp.ones_like(gate))
    stat1[me, n_exp + 1 : n_exp + 2, :] = by_kind(entropy)

    def s1_copy(i):
        return pltpu.make_async_remote_copy(
            src_ref=stat1.at[i], dst_ref=stat1.at[i], send_sem=s1_send,
            recv_sem=s1_recv.at[i], device_id={"expert": lead}, device_id_type=MESH,
        )

    def s2_copy(k):
        return pltpu.make_async_remote_copy(
            src_ref=stat2.at[me_dp], dst_ref=stat2.at[me_dp], send_sem=s2_send.at[k],
            recv_sem=s2_recv.at[k], device_id={"dp": peers_dp[k]}, device_id_type=MESH,
        )

    def s3_copy(k):
        return pltpu.make_async_remote_copy(
            src_ref=stat3, dst_ref=stat3, send_sem=s3_send.at[k], recv_sem=s3_recv,
            device_id={"expert": k}, device_id_type=MESH,
        )

    @pl.when(me != lead)
    def _():
        s1_copy(me).start()

    def first_sums():
        @pl.when(me == lead)
        def _():
            for i in others:
                s1_copy(i).wait_recv()
            stat2[me_dp] = sum(stat1[i] for i in range(n))
            pl.semaphore_wait(barrier, n_dp - 1)
            for k in range(1, n_dp):
                s2_copy(k).start()

    def last_sums():
        @pl.when(me == lead)
        def _():
            for k in range(1, n_dp):
                s2_copy(k).wait()
            stat3[...] = sum(stat2[i] for i in range(n_dp))
            for k in others:
                s3_copy(k).start()
            for k in others:
                s3_copy(k).wait_send()

        @pl.when(me != lead)
        def _():
            s1_copy(me).wait_send()
            s3_copy(0).wait_recv()

    def experts(start, count, first):
        for j in range(n1):
            if first:
                w1_copy(j).wait()
            act = gelu(
                jnp.dot(recv[start : start + count, :], w1[j], preferred_element_type=jnp.float32)
            )
            hidden[0:count, pl.ds(j * c1, c1)] = act.astype(jnp.bfloat16)
        for j in range(n2):
            if first:
                w2_copy(j).wait()
            res[start : start + count, pl.ds(j * c2, c2)] = jnp.dot(
                hidden[0:count, :], w2[j], preferred_element_type=jnp.float32
            ).astype(jnp.bfloat16)

    lanes = lax.broadcasted_iota(jnp.int32, picks.shape, 1)
    picks[...] = jnp.where(lanes == 0, to_columns(label.astype(jnp.float32)), to_columns(gate))
    stores = [pltpu.make_async_copy(picks, picks_hbm, out_sem.at[0])]
    for store in stores:
        store.start()

    for c in range(chunks):
        for k in range(1, n):
            out_copy(c, k).wait_recv()
        if c == 0:
            experts(0, cap + spans[c], True)
        else:
            experts(bases[c], spans[c], False)
        start_all(back_copy, c)
        if c == 0:
            stores.append(
                pltpu.make_async_copy(res.at[pl.ds(0, cap)], ret.at[pl.ds(0, cap)], out_sem.at[1])
            )
            stores[-1].start()
            first_sums()

    last_sums()
    totals = jnp.transpose(stat3[...])
    denom = jnp.maximum(totals[0:2, n_exp : n_exp + 1], 1.0)
    mean = totals[0:2, 0:n_exp] / denom
    importance[...] = mean
    logs = jnp.log(jnp.where(mean == 0.0, 1.0, mean))
    entropies[:, 0:1] = totals[0:2, n_exp + 1 : n_exp + 2] / denom
    entropies[:, 1:2] = -jnp.sum(mean * logs, axis=1, keepdims=True)
    stores.append(pltpu.make_async_copy(importance, importance_hbm, out_sem.at[2]))
    stores.append(pltpu.make_async_copy(entropies, entropies_hbm, out_sem.at[3]))
    for store in stores[-2:]:
        store.start()

    for c in range(chunks):
        for k in range(1, n):
            out_copy(c, k).wait_send()
            back_copy(c, k).wait()
    for store in stores:
        store.wait()


def combine(
    ret_hbm, picks_hbm, importance_in, entropies_in, mixed_hbm, importance_hbm, entropies_hbm,
    ret, picks, importance, entropies, mixed, in_sem, out_sem,
):
    blocks, n_rows, step = ret.shape
    columns = [pl.ds(j * step, step) for j in range(blocks)]
    pairs = (
        (picks_hbm, picks), (importance_in, importance), (entropies_in, entropies),
        *((ret_hbm.at[:, columns[j]], ret.at[j]) for j in range(blocks)),
    )
    loads = [pltpu.make_async_copy(a, b, in_sem.at[i]) for i, (a, b) in enumerate(pairs)]
    pairs = (
        (importance, importance_hbm), (entropies, entropies_hbm),
        *((mixed.at[j], mixed_hbm.at[:, columns[j]]) for j in range(blocks)),
    )
    stores = [pltpu.make_async_copy(a, b, out_sem.at[i]) for i, (a, b) in enumerate(pairs)]
    for load in loads:
        load.start()
    for i in range(3):
        loads[i].wait()
    for i in range(2):
        stores[i].start()
    lanes = lax.broadcasted_iota(jnp.int32, (picks.shape[0], n_rows), 1).astype(jnp.float32)
    take = jnp.where(lanes == picks[:, 0:1], 1.0, 0.0).astype(jnp.bfloat16)
    for j in range(blocks):
        loads[3 + j].wait()
        rows = jnp.dot(take, ret[j], preferred_element_type=jnp.float32)
        mixed[j] = (picks[:, 1:2] * rows).astype(jnp.bfloat16)
        stores[2 + j].start()
    for store in stores:
        store.wait()


def per_device(n, n_dp, tokens, router, w_in, w_out, assign, modality, slot):
    n_tok, width = tokens.shape
    n_exp = router.shape[1]
    ff = w_in.shape[2]
    cap = -(-(3 * n_tok // (2 * n_exp)) // 16) * 16
    units = cap // 16
    parts = [16 * size for size in (1, units - 1 - units // 3, units // 3) if size]
    chunks = len(parts)
    rows = n * cap
    c1, c2 = min(ff, 512), min(width, 256)
    stat_rows = -(-(n_exp + 2) // 8) * 8
    hbm = pl.BlockSpec(memory_space=pltpu.HBM)
    dma = pltpu.SemaphoreType.DMA
    block = pltpu.VMEM((rows, width), jnp.bfloat16)
    f32, bf16 = jnp.float32, jnp.bfloat16
    stats_shape = [jax.ShapeDtypeStruct((2, n_exp), f32), jax.ShapeDtypeStruct((2, 2), f32)]
    mixed_shape = jax.ShapeDtypeStruct((n_tok, width), bf16)
    carried = [
        jax.ShapeDtypeStruct((rows, width), bf16),
        jax.ShapeDtypeStruct((n_tok, 128), f32),
        *stats_shape,
    ]
    results = pl.pallas_call(
        functools.partial(kernel, n, n_dp, cap, parts),
        out_shape=carried,
        in_specs=[hbm] * 7,
        out_specs=[hbm] * 4,
        scratch_shapes=[
            *[pltpu.VMEM(out.shape, out.dtype) for out in carried[1:]],
            pltpu.VMEM((n_tok, width), jnp.bfloat16),
            pltpu.VMEM((n_exp, width), jnp.bfloat16),
            pltpu.VMEM((1, n_tok), jnp.int32),
            pltpu.VMEM((1, n_tok), jnp.int32),
            pltpu.VMEM((1, n_tok), jnp.int32),
            pltpu.VMEM((ff // c1, width, c1), jnp.bfloat16),
            pltpu.VMEM((width // c2, ff, c2), jnp.bfloat16),
            block, block, block,
            pltpu.VMEM((rows, ff), jnp.bfloat16),
            pltpu.VMEM((n, stat_rows, 128), jnp.float32),
            pltpu.VMEM((n_dp, stat_rows, 128), jnp.float32),
            pltpu.VMEM((stat_rows, 128), jnp.float32),
            dma((5,)), dma((4,)), dma((ff // c1,)), dma((width // c2,)),
            dma((chunks, n)), dma((chunks, n)), dma((chunks, n)), dma((chunks, n)),
            dma, dma((n,)), dma((n_dp,)), dma((n_dp,)), dma((n,)), dma,
            pltpu.SemaphoreType.REGULAR((n,)),
        ],
        compiler_params=pltpu.CompilerParams(
            collective_id=0, has_side_effects=True, vmem_limit_bytes=VMEM_LIMIT
        ),
        cost_estimate=pl.CostEstimate(
            flops=4 * rows * width * ff, bytes_accessed=4 * width * ff, transcendentals=rows * ff
        ),
    )(
        tokens, router.T, w_in, w_out,
        assign.reshape(1, n_tok), modality.reshape(1, n_tok), slot.reshape(1, n_tok),
    )
    blocks = width // c2
    return pl.pallas_call(
        combine,
        out_shape=[mixed_shape, *stats_shape],
        in_specs=[hbm] * 4,
        out_specs=[hbm] * 3,
        scratch_shapes=[
            pltpu.VMEM((blocks, rows, c2), bf16),
            *[pltpu.VMEM(out.shape, out.dtype) for out in carried[1:]],
            pltpu.VMEM((blocks, n_tok, c2), bf16),
            dma((3 + blocks,)), dma((2 + blocks,)),
        ],
        compiler_params=pltpu.CompilerParams(vmem_limit_bytes=VMEM_LIMIT),
    )(*results)


def solution(mesh):
    return jax.shard_map(
        functools.partial(per_device, mesh.shape["expert"], mesh.shape["dp"]),
        mesh=mesh,
        in_specs=(
            P(("dp", "expert"), None),
            P(),
            P("expert", None, None),
            P("expert", None, None),
            P(("dp", "expert")),
            P(("dp", "expert")),
            P(("dp", "expert")),
        ),
        out_specs=(P(("dp", "expert"), None), P(), P()),
        check_vma=False,
    )
```

```python
import functools
import math

import jax
import jax.numpy as jnp
from jax import lax
from jax.experimental import pallas as pl
from jax.experimental.pallas import tpu as pltpu
from jax.sharding import PartitionSpec as P

MESH = pl.DeviceIdType.MESH
VMEM_LIMIT = 63 * 2**20


def partner(me, k, n):
    out, bit = 0, 1
    while bit < n:
        digit = lax.rem(lax.div(me, bit), 2)
        if k & bit:
            digit = 1 - digit
        out = out + digit * bit
        bit *= 2
    return out


def gelu(x):
    scale = math.sqrt(2.0 / math.pi)
    half = 0.5 * x
    return half + half * jnp.tanh(x * (scale + (scale * 0.044715) * (x * x)))


def to_columns(row):
    return jnp.transpose(jnp.broadcast_to(row, (128, row.shape[1])))


def kernel(
    n, n_dp, cap, parts,
    tokens_hbm, router_hbm, w_in_hbm, w_out_hbm, assign_hbm, modality_hbm, slot_hbm,
    ret, picks_hbm, importance_hbm, entropies_hbm,
    picks, importance, entropies, tokens, router_t, assign, modality, slot, w1, w2, buf, recv, res, hidden, stat1, stat2, stat3,
    in_sem, out_sem, w1_sem, w2_sem, out_send, out_recv, back_send, back_recv, s1_send, s1_recv, s2_send, s2_recv,
    s3_send, s3_recv, entered,
):
    me = lax.axis_index("expert")
    me_dp = lax.axis_index("dp")
    lead = 0
    others = range(1, n)
    peers = [partner(me, k, n) for k in range(n)]
    peers_dp = [partner(me_dp, k, n_dp) for k in range(n_dp)]
    n_tok, width = tokens.shape
    n_exp = router_t.shape[0]
    starts = [sum(parts[:c]) for c in range(len(parts))]
    bases = [cap + (n - 1) * start for start in starts]
    spans = [(n - 1) * part for part in parts]
    chunks = len(parts)

    barrier = pltpu.get_barrier_semaphore()
    for k in range(1, n):
        @pl.when(me != lead ^ k)
        def _():
            pl.semaphore_signal(
                barrier, inc=1, device_id={"expert": peers[k]}, device_id_type=MESH
            )

    @pl.when(me == lead)
    def _():
        for k in range(1, n_dp):
            pl.semaphore_signal(
                barrier, inc=1, device_id={"dp": peers_dp[k]}, device_id_type=MESH
            )

    pairs = (
        (assign_hbm, assign), (slot_hbm, slot), (tokens_hbm, tokens),
        (router_hbm, router_t), (modality_hbm, modality),
    )
    loads = [pltpu.make_async_copy(a, b, in_sem.at[i]) for i, (a, b) in enumerate(pairs)]
    for load in loads:
        load.start()

    def greet_group():
        @pl.when(me != lead)
        def _():
            pl.semaphore_wait(barrier, n - 1)
            pl.semaphore_signal(
                entered.at[me], inc=1, device_id={"expert": lead}, device_id_type=MESH
            )

    def await_member(k):
        @pl.when(me == lead)
        def _():
            pl.semaphore_wait(entered.at[k], 1)

    greet_group()
    n1, n2 = w1.shape[0], w2.shape[0]
    c1, c2 = w1.shape[2], w2.shape[2]

    def w1_copy(j):
        return pltpu.make_async_copy(w_in_hbm.at[0, :, pl.ds(j * c1, c1)], w1.at[j], w1_sem.at[j])

    def w2_copy(j):
        return pltpu.make_async_copy(w_out_hbm.at[0, :, pl.ds(j * c2, c2)], w2.at[j], w2_sem.at[j])

    loads[0].wait()
    loads[1].wait()
    rel = jnp.bitwise_xor(assign[...], me)
    where_slot = slot[...]
    label = where_slot
    for start, base, part in zip(starts, bases, parts):
        inside = jnp.logical_and(rel > 0, where_slot >= start)
        label = jnp.where(inside, base + (rel - 1) * part + where_slot - start, label)

    def place(dst, start, count):
        rows = lax.broadcasted_iota(jnp.int32, (count, n_tok), 0) + start
        one_hot = jnp.where(rows == label, 1.0, 0.0).astype(jnp.bfloat16)
        dst[start : start + count, :] = jnp.dot(
            one_hot, tokens[...], preferred_element_type=jnp.float32
        ).astype(jnp.bfloat16)

    def rows_of(c, k):
        return pl.ds(bases[c] + (k - 1) * parts[c], parts[c])

    def send(src, dst, sems, c, k):
        rows = rows_of(c, k)
        return pltpu.make_async_remote_copy(
            src_ref=src.at[rows], dst_ref=dst.at[rows],
            send_sem=sems[0].at[c, k], recv_sem=sems[1].at[c, k],
            device_id={"expert": peers[k]}, device_id_type=MESH,
        )

    def out_copy(c, k):
        return send(buf, recv, (out_send, out_recv), c, k)

    def back_copy(c, k):
        return send(res, ret, (back_send, back_recv), c, k)

    loads[2].wait()
    for j in range(n1):
        w1_copy(j).start()
    for j in range(n2):
        w2_copy(j).start()
    for c in range(chunks):
        place(buf, bases[c], spans[c])
        for k in reversed(range(1, n)):
            if c == 0:
                await_member(k)
            out_copy(c, k).start()
    place(recv, 0, cap)

    loads[3].wait()
    loads[4].wait()
    logits = lax.dot_general(
        router_t[...], tokens[...], (((1,), (1,)), ((), ())), preferred_element_type=jnp.float32
    )
    shifted = logits - jnp.max(logits, axis=0, keepdims=True)
    unnorm = jnp.exp(shifted)
    total = jnp.sum(unnorm, axis=0, keepdims=True)
    probs = unnorm / total
    logp = shifted - jnp.log(total)
    picked = lax.broadcasted_iota(jnp.int32, probs.shape, 0) == assign[...]
    gate = jnp.sum(jnp.where(picked, probs, 0.0), axis=0, keepdims=True)
    entropy = -jnp.sum(probs * logp, axis=0, keepdims=True)
    kinds = [(modality[...] == m).astype(jnp.float32) for m in range(2)]

    def by_kind(values):
        first, second = (jnp.sum(values * kind, axis=1, keepdims=True) for kind in kinds)
        lane = lax.broadcasted_iota(jnp.int32, (values.shape[0], 128), 1)
        return jnp.where(lane == 0, first, jnp.where(lane == 1, second, 0.0))

    stat1[me] = jnp.zeros(stat1.shape[1:], jnp.float32)
    stat1[me, 0:n_exp, :] = by_kind(probs)
    stat1[me, n_exp : n_exp + 1, :] = by_kind(jnp.ones_like(gate))
    stat1[me, n_exp + 1 : n_exp + 2, :] = by_kind(entropy)

    def s1_copy(i):
        return pltpu.make_async_remote_copy(
            src_ref=stat1.at[i], dst_ref=stat1.at[i], send_sem=s1_send,
            recv_sem=s1_recv.at[i], device_id={"expert": lead}, device_id_type=MESH,
        )

    def s2_copy(k):
        return pltpu.make_async_remote_copy(
            src_ref=stat2.at[me_dp], dst_ref=stat2.at[me_dp], send_sem=s2_send.at[k],
            recv_sem=s2_recv.at[k], device_id={"dp": peers_dp[k]}, device_id_type=MESH,
        )

    def s3_copy(k):
        return pltpu.make_async_remote_copy(
            src_ref=stat3, dst_ref=stat3, send_sem=s3_send.at[k], recv_sem=s3_recv,
            device_id={"expert": k}, device_id_type=MESH,
        )

    @pl.when(me != lead)
    def _():
        s1_copy(me).start()

    def first_sums():
        @pl.when(me == lead)
        def _():
            for i in others:
                s1_copy(i).wait_recv()
            stat2[me_dp] = sum(stat1[i] for i in range(n))
            pl.semaphore_wait(barrier, n_dp - 1)
            for k in range(1, n_dp):
                s2_copy(k).start()

    def last_sums():
        @pl.when(me == lead)
        def _():
            for k in range(1, n_dp):
                s2_copy(k).wait()
            stat3[...] = sum(stat2[i] for i in range(n_dp))
            for k in others:
                s3_copy(k).start()
            for k in others:
                s3_copy(k).wait_send()

        @pl.when(me != lead)
        def _():
            s1_copy(me).wait_send()
            s3_copy(0).wait_recv()

    def experts(start, count, first):
        for j in range(n1):
            if first:
                w1_copy(j).wait()
            act = gelu(
                jnp.dot(recv[start : start + count, :], w1[j], preferred_element_type=jnp.float32)
            )
            hidden[0:count, pl.ds(j * c1, c1)] = act.astype(jnp.bfloat16)
        for j in range(n2):
            if first:
                w2_copy(j).wait()
            res[start : start + count, pl.ds(j * c2, c2)] = jnp.dot(
                hidden[0:count, :], w2[j], preferred_element_type=jnp.float32
            ).astype(jnp.bfloat16)

    lanes = lax.broadcasted_iota(jnp.int32, picks.shape, 1)
    picks[...] = jnp.where(lanes == 0, to_columns(label.astype(jnp.float32)), to_columns(gate))
    stores = [pltpu.make_async_copy(picks, picks_hbm, out_sem.at[0])]
    for store in stores:
        store.start()

    for c in range(chunks):
        for k in range(1, n):
            out_copy(c, k).wait_recv()
        if c == 0:
            experts(0, cap + spans[c], True)
        else:
            experts(bases[c], spans[c], False)
        for k in reversed(range(1, n)):
            back_copy(c, k).start()
        if c == 0:
            stores.append(
                pltpu.make_async_copy(res.at[pl.ds(0, cap)], ret.at[pl.ds(0, cap)], out_sem.at[1])
            )
            stores[-1].start()
            first_sums()

    last_sums()
    totals = jnp.transpose(stat3[...])
    denom = jnp.maximum(totals[0:2, n_exp : n_exp + 1], 1.0)
    mean = totals[0:2, 0:n_exp] / denom
    importance[...] = mean
    logs = jnp.log(jnp.where(mean == 0.0, 1.0, mean))
    entropies[:, 0:1] = totals[0:2, n_exp + 1 : n_exp + 2] / denom
    entropies[:, 1:2] = -jnp.sum(mean * logs, axis=1, keepdims=True)
    stores.append(pltpu.make_async_copy(importance, importance_hbm, out_sem.at[2]))
    stores.append(pltpu.make_async_copy(entropies, entropies_hbm, out_sem.at[3]))
    for store in stores[-2:]:
        store.start()

    for c in range(chunks):
        for k in range(1, n):
            out_copy(c, k).wait_send()
            back_copy(c, k).wait()
    for store in stores:
        store.wait()


def combine(
    ret_hbm, picks_hbm, importance_in, entropies_in, mixed_hbm, importance_hbm, entropies_hbm,
    ret, picks, importance, entropies, mixed, in_sem, out_sem,
):
    blocks, n_rows, step = ret.shape
    columns = [pl.ds(j * step, step) for j in range(blocks)]
    pairs = (
        (picks_hbm, picks), (importance_in, importance), (entropies_in, entropies),
        *((ret_hbm.at[:, columns[j]], ret.at[j]) for j in range(blocks)),
    )
    loads = [pltpu.make_async_copy(a, b, in_sem.at[i]) for i, (a, b) in enumerate(pairs)]
    pairs = (
        (importance, importance_hbm), (entropies, entropies_hbm),
        *((mixed.at[j], mixed_hbm.at[:, columns[j]]) for j in range(blocks)),
    )
    stores = [pltpu.make_async_copy(a, b, out_sem.at[i]) for i, (a, b) in enumerate(pairs)]
    for load in loads:
        load.start()
    for i in range(3):
        loads[i].wait()
    for i in range(2):
        stores[i].start()
    lanes = lax.broadcasted_iota(jnp.int32, (picks.shape[0], n_rows), 1).astype(jnp.float32)
    take = jnp.where(lanes == picks[:, 0:1], 1.0, 0.0).astype(jnp.bfloat16)
    for j in range(blocks):
        loads[3 + j].wait()
        rows = jnp.dot(take, ret[j], preferred_element_type=jnp.float32)
        mixed[j] = (picks[:, 1:2] * rows).astype(jnp.bfloat16)
        stores[2 + j].start()
    for store in stores:
        store.wait()


def per_device(n, n_dp, tokens, router, w_in, w_out, assign, modality, slot):
    n_tok, width = tokens.shape
    n_exp = router.shape[1]
    ff = w_in.shape[2]
    cap = -(-(3 * n_tok // (2 * n_exp)) // 16) * 16
    units = cap // 16
    parts = [16 * size for size in (1, units - 1 - units // 3, units // 3) if size]
    chunks = len(parts)
    rows = n * cap
    c1, c2 = min(ff, 512), min(width, 256)
    stat_rows = -(-(n_exp + 2) // 8) * 8
    hbm = pl.BlockSpec(memory_space=pltpu.HBM)
    dma = pltpu.SemaphoreType.DMA
    block = pltpu.VMEM((rows, width), jnp.bfloat16)
    f32, bf16 = jnp.float32, jnp.bfloat16
    stats_shape = [jax.ShapeDtypeStruct((2, n_exp), f32), jax.ShapeDtypeStruct((2, 2), f32)]
    mixed_shape = jax.ShapeDtypeStruct((n_tok, width), bf16)
    carried = [
        jax.ShapeDtypeStruct((rows, width), bf16),
        jax.ShapeDtypeStruct((n_tok, 128), f32),
        *stats_shape,
    ]
    results = pl.pallas_call(
        functools.partial(kernel, n, n_dp, cap, parts),
        out_shape=carried,
        in_specs=[hbm] * 7,
        out_specs=[hbm] * 4,
        scratch_shapes=[
            *[pltpu.VMEM(out.shape, out.dtype) for out in carried[1:]],
            pltpu.VMEM((n_tok, width), jnp.bfloat16),
            pltpu.VMEM((n_exp, width), jnp.bfloat16),
            pltpu.VMEM((1, n_tok), jnp.int32),
            pltpu.VMEM((1, n_tok), jnp.int32),
            pltpu.VMEM((1, n_tok), jnp.int32),
            pltpu.VMEM((ff // c1, width, c1), jnp.bfloat16),
            pltpu.VMEM((width // c2, ff, c2), jnp.bfloat16),
            block, block, block,
            pltpu.VMEM((rows, ff), jnp.bfloat16),
            pltpu.VMEM((n, stat_rows, 128), jnp.float32),
            pltpu.VMEM((n_dp, stat_rows, 128), jnp.float32),
            pltpu.VMEM((stat_rows, 128), jnp.float32),
            dma((5,)), dma((4,)), dma((ff // c1,)), dma((width // c2,)),
            dma((chunks, n)), dma((chunks, n)), dma((chunks, n)), dma((chunks, n)),
            dma, dma((n,)), dma((n_dp,)), dma((n_dp,)), dma((n,)), dma,
            pltpu.SemaphoreType.REGULAR((n,)),
        ],
        compiler_params=pltpu.CompilerParams(
            collective_id=0, has_side_effects=True, vmem_limit_bytes=VMEM_LIMIT
        ),
        cost_estimate=pl.CostEstimate(
            flops=4 * rows * width * ff, bytes_accessed=4 * width * ff, transcendentals=rows * ff
        ),
    )(
        tokens, router.T, w_in, w_out,
        assign.reshape(1, n_tok), modality.reshape(1, n_tok), slot.reshape(1, n_tok),
    )
    blocks = width // c2
    return pl.pallas_call(
        combine,
        out_shape=[mixed_shape, *stats_shape],
        in_specs=[hbm] * 4,
        out_specs=[hbm] * 3,
        scratch_shapes=[
            pltpu.VMEM((blocks, rows, c2), bf16),
            *[pltpu.VMEM(out.shape, out.dtype) for out in carried[1:]],
            pltpu.VMEM((blocks, n_tok, c2), bf16),
            dma((3 + blocks,)), dma((2 + blocks,)),
        ],
        compiler_params=pltpu.CompilerParams(vmem_limit_bytes=VMEM_LIMIT),
    )(*results)


def solution(mesh):
    return jax.shard_map(
        functools.partial(per_device, mesh.shape["expert"], mesh.shape["dp"]),
        mesh=mesh,
        in_specs=(
            P(("dp", "expert"), None),
            P(),
            P("expert", None, None),
            P("expert", None, None),
            P(("dp", "expert")),
            P(("dp", "expert")),
            P(("dp", "expert")),
        ),
        out_specs=(P(("dp", "expert"), None), P(), P()),
        check_vma=False,
    )
```
